128 devices in a mesh: seq: 16 (over x_hi, y, core), head: 8 (over z, x_lo).
Axes of the slice: x: 4 (x_hi: 2, x_lo: 2; x = x_hi * 2 + x_lo), y: 4, z: 4, core: 2. Of those that a mesh axis runs over, the one named last changes fastest.
Arguments:
- query: bfloat16 [4096, 4096], P('seq', 'head'), may hold values from -30 to 30
- key_rows: bfloat16 [4096, 4096], P('seq', 'head'), may hold values from -4 to 4
- value_rows: bfloat16 [4096, 4096], P('seq', 'head'), may hold values from -6 to 6
- out_grad: bfloat16 [4096, 4096], P('seq', 'head'), may hold values from -6 to 6
- sample_blocks: int32 [3], replicated, may hold values from 1 to 20, as said below
Outputs:
- query_grad: bfloat16 [4096, 4096], P('seq', 'head')
- key_grad: bfloat16 [4096, 4096], P('seq', 'head')
- value_grad: bfloat16 [4096, 4096], P('seq', 'head')
The draws below stay inside these ranges and needn't reach their ends.
Inputs may be any that keep to these rules, and one draw needn't show every extreme that they name: `sample_blocks`: the 3 samples lie one after another in the pack, each a whole number of 128-token blocks, together all 32 blocks; one sample has exactly 16 + max(1, 4) blocks.
All inputs are finite; a program needn't handle non-finite values.
Results may differ from the reference program's by a relative error of at most 0.005.
Values may be sent and summed in bfloat16 or wider, within the bound.
A program may use at most 64 MiB of HBM per device.

```python
import jax
import jax.numpy as jnp
from jax import lax

HEADS = 32
HD = 128
BLK = 128
TOKENS = 4096
BLOCKS = 32


def draw_query(key, part):
    key = jax.random.fold_in(key, 7)
    values = jnp.clip(jax.random.normal(key, (TOKENS, HEADS * HD), jnp.float32), -4.0, 4.0)
    return values.astype(jnp.bfloat16)


def draw_key_rows(key, part):
    key = jax.random.fold_in(key, 9)
    values = jnp.clip(jax.random.normal(key, (TOKENS, HEADS * HD), jnp.float32), -4.0, 4.0)
    return values.astype(jnp.bfloat16)


def draw_sample_blocks(key, part):
    key = jax.random.fold_in(key, 21)
    largest = BLOCKS // 2 + max(1, BLOCKS // 8)
    remainder = BLOCKS - largest
    first_small = jax.random.randint(jax.random.fold_in(key, 1), (), 1, remainder, dtype=jnp.int32)
    big_place = jax.random.randint(jax.random.fold_in(key, 2), (), 0, 3, dtype=jnp.int32)
    places = jnp.arange(3, dtype=jnp.int32)
    small_rank = places - (places > big_place).astype(jnp.int32)
    small_size = jnp.where(small_rank == 0, first_small, remainder - first_small)
    return jnp.where(places == big_place, jnp.int32(largest), small_size).astype(jnp.int32)


def levels(stream_key, shape, shards, smallest, top_value):
    factor_of, own = 1.0, jax.random.fold_in(stream_key, 6)
    for dim, shards_of in shards:
        heights = jnp.exp(jax.random.uniform(jax.random.fold_in(own, dim), (shards_of,), jnp.float32, smallest / len(shards), top_value / len(shards)))
        factor_of = factor_of * jnp.repeat(heights, shape[dim] // shards_of).reshape([-1 if axis == dim else 1 for axis in range(len(shape))])
    return factor_of


def centred(stream_key, shape, spread, bound, shards=(), kind=jnp.bfloat16):
    entries = jax.random.normal(stream_key, shape, jnp.float32) * spread
    if len(shards) > 0:
        entries = levels(stream_key, shape, shards, -0.22, 0.18) * entries
    return jnp.clip(entries, min=-bound, max=bound).astype(kind)


def setup_inputs(seed: int = 0) -> dict:
    splits = jax.random.split(jax.random.key(seed), 6)
    query = draw_query(jax.random.fold_in(splits[5], 71), 0)
    key_rows = draw_key_rows(jax.random.fold_in(splits[5], 71), 0)
    value_rows = centred(splits[2], (TOKENS, HEADS * HD), 1.0, 6.0, ((0, 16), (1, 8)))
    out_grad = centred(splits[3], (TOKENS, HEADS * HD), 1.0, 6.0, ((0, 16), (1, 8)))
    sample_blocks = draw_sample_blocks(jax.random.fold_in(splits[5], 71), 0)
    return {"query": query, "key_rows": key_rows, "value_rows": value_rows, "out_grad": out_grad, "sample_blocks": sample_blocks}


masked_fill = -1e30


def reference(query, key_rows, value_rows, out_grad, sample_blocks):
    scaling = HD ** -0.5
    sample_ends = jnp.cumsum(sample_blocks)
    block_index = jnp.arange(TOKENS, dtype=jnp.int32) // BLK
    segment = jnp.sum((block_index[:, None] >= sample_ends[None, :]).astype(jnp.int32), axis=1)
    allowed = segment[:, None] == segment[None, :]

    def by_heads(stacked):
        return stacked.reshape(TOKENS, HEADS, HD).transpose(1, 0, 2)

    def back_rows(stacked):
        return stacked.transpose(1, 0, 2).reshape(TOKENS, HEADS * HD)

    def one_head(operands):
        query_head, key_head, value_head, grad_head = operands
        scores = jnp.dot(query_head, key_head.T, preferred_element_type=jnp.float32) * scaling
        row_max = jnp.max(jnp.where(allowed, scores, masked_fill), axis=1, keepdims=True)
        exp_terms = jnp.where(allowed, jnp.exp(scores - row_max), 0.0)
        probability = exp_terms / jnp.sum(exp_terms, axis=1, keepdims=True)
        prob_grad = jnp.dot(grad_head, value_head.T, preferred_element_type=jnp.float32)
        delta = jnp.sum(probability * prob_grad, axis=1, keepdims=True)
        score_grad = probability * (prob_grad - delta)
        score_low = score_grad.astype(jnp.bfloat16)
        prob_low = probability.astype(jnp.bfloat16)
        query_part = (jnp.dot(score_low, key_head, preferred_element_type=jnp.float32) * scaling).astype(jnp.bfloat16)
        key_part = (jnp.dot(score_low.T, query_head, preferred_element_type=jnp.float32) * scaling).astype(jnp.bfloat16)
        value_part = jnp.dot(prob_low.T, grad_head, preferred_element_type=jnp.float32).astype(jnp.bfloat16)
        return (query_part, key_part, value_part)

    head_grads = lax.map(one_head, (by_heads(query), by_heads(key_rows), by_heads(value_rows), by_heads(out_grad)))
    return (back_rows(head_grads[0]), back_rows(head_grads[1]), back_rows(head_grads[2]))
```

```python
import functools

import jax
import jax.numpy as jnp
from jax import lax
from jax.experimental import pallas as pl
from jax.experimental.pallas import tpu as pltpu
from jax.sharding import PartitionSpec as P

HD = 128
BLK = 128
ROWS = 256
MESH = pl.DeviceIdType.MESH
SCALE = HD**-0.5
LOG2E = 1.4426950408889634
BF16 = jnp.bfloat16
F32 = jnp.float32


def place():
    s = lax.axis_index("seq")
    return lax.div(s, 8), lax.rem(lax.div(s, 2), 4), lax.rem(s, 2)


def seq_id(x, y, c):
    return {"seq": x * 8 + y * 2 + c}


def meet(peers):
    barrier = pltpu.get_barrier_semaphore()
    for peer in peers:
        pl.semaphore_signal(barrier, inc=1, device_id=peer, device_id_type=MESH)
    pl.semaphore_wait(barrier, len(peers))


def gather_kernel(q, k, v, g, qg, kv, y_send, y_recv, x_send, x_recv, c_send, c_recv, own):
    x, y, c = place()
    x_peer, c_peer = seq_id(1 - x, y, c), seq_id(x, y, 1 - c)
    y_of = lambda d: lax.rem(y + d, 4)
    meet([x_peer, c_peer] + [seq_id(x, y_of(d), c) for d in (1, 2, 3)])

    def chunk(xx, yy, cc):
        return xx * 8 + yy * 2 + cc

    def cols(ref, head):
        return ref.at[:, pl.ds(pl.multiple_of(head * HD, HD), HD)]

    def remote(src, dst, send, recv, device):
        return pltpu.make_async_remote_copy(
            src_ref=src, dst_ref=dst, send_sem=send, recv_sem=recv, device_id=device, device_id_type=MESH
        )

    sends = []

    def go(copy):
        copy.start()
        sends.append(copy)

    here = chunk(x, y, c)
    own_copies = [
        pltpu.make_async_copy(cols(k, y), kv.at[here, 0], own.at[0]),
        pltpu.make_async_copy(cols(v, y), kv.at[here, 1], own.at[1]),
        pltpu.make_async_copy(cols(q, y), qg.at[y, 0], own.at[2]),
        pltpu.make_async_copy(cols(g, y), qg.at[y, 1], own.at[3]),
    ]
    for copy in own_copies:
        copy.start()
    for a, ref in enumerate((k, v)):
        for d in (1, 3, 2):
            go(remote(cols(ref, y_of(d)), kv.at[here, a], y_send.at[a, d], y_recv.at[a, d], seq_id(x, y_of(d), c)))
    for copy in own_copies[:2]:
        copy.wait()

    def onward(d):
        there = chunk(x, y_of(d), c)
        go(remote(kv.at[there], kv.at[there], x_send.at[d], x_recv.at[d], x_peer))
        go(remote(kv.at[there], kv.at[there], c_send.at[0, d], c_recv.at[0, d], c_peer))

    onward(0)
    for a, ref in enumerate((q, g)):
        for d in (1, 3, 2):
            go(remote(cols(ref, y_of(d)), qg.at[y, a], y_send.at[a + 2, d], y_recv.at[a + 2, d], seq_id(x, y_of(d), c)))

    def arrived(dst, recv):
        remote(dst, dst, own.at[0], recv, x_peer).wait_recv()

    for d in (3, 1, 2):
        there = chunk(x, y_of(d), c)
        for a in range(2):
            arrived(kv.at[there, a], y_recv.at[a, 4 - d])
        onward(d)
    for d in (0, 3, 1, 2):
        there = chunk(1 - x, y_of(d), c)
        arrived(kv.at[there], x_recv.at[d])
        go(remote(kv.at[there], kv.at[there], c_send.at[1, d], c_recv.at[1, d], c_peer))
    for d in (3, 1, 2):
        for a in range(2):
            arrived(qg.at[y_of(d), a], y_recv.at[a + 2, 4 - d])
    for d in range(4):
        arrived(kv.at[chunk(x, y_of(d), 1 - c)], c_recv.at[0, d])
        arrived(kv.at[chunk(1 - x, y_of(d), 1 - c)], c_recv.at[1, d])
    for copy in own_copies[2:]:
        copy.wait()
    for copy in sends:
        copy.wait_send()


def gather(q, k, v, g):
    dma = pltpu.SemaphoreType.DMA
    return pl.pallas_call(
        gather_kernel,
        out_shape=(
            jax.ShapeDtypeStruct((4, 2, ROWS, HD), BF16),
            jax.ShapeDtypeStruct((16, 2, ROWS, HD), BF16),
        ),
        in_specs=[pl.BlockSpec(memory_space=pl.ANY)] * 4,
        out_specs=(pl.BlockSpec(memory_space=pl.ANY),) * 2,
        scratch_shapes=[
            dma((4, 4)), dma((4, 4)), dma((4,)), dma((4,)), dma((2, 4)), dma((2, 4)), dma((4,)),
        ],
        compiler_params=pltpu.CompilerParams(collective_id=0, has_side_effects=True),
        name="exchange_in",
    )(q, k, v, g)


def grads_kernel(blocks, qg, kv, dq_out, dkv_out, s_buf, d_buf, dkv_acc):
    x, y, c = place()
    end0 = blocks[0]
    end1 = end0 + blocks[1]

    def seg(b):
        return (b >= end0).astype(jnp.int32) + (b >= end1).astype(jnp.int32)

    dkv_acc[...] = jnp.zeros_like(dkv_acc)
    lane = lax.broadcasted_iota(jnp.int32, (1, ROWS), 1)
    nt = (((1,), (1,)), ((), ()))
    tn = (((0,), (0,)), ((), ()))

    def of_chunk(i, carry):
        b0 = 16 * x + 4 * i + 2 * c
        seg0, seg1 = seg(b0), seg(b0 + 1)
        start = jnp.where(seg0 == 0, 0, jnp.where(seg0 == 1, end0, end1))
        stop = jnp.where(seg1 == 0, end0, jnp.where(seg1 == 1, end1, 32))
        lo, hi = lax.div(start, 2), lax.div(stop + 1, 2)
        lane_seg = jnp.where(lane < BLK, seg0, seg1)
        q_i, g_i = qg[i, 0], qg[i, 1]

        def scores(j, m):
            s_t = lax.dot_general(kv[j, 0], q_i, nt, preferred_element_type=F32)
            s_buf[j] = s_t
            for half in range(2):
                top = jnp.max(s_t[half * BLK : (half + 1) * BLK], axis=0, keepdims=True)
                m = jnp.maximum(m, jnp.where(lane_seg == seg(2 * j + half), top, -1e30))
            return m

        m = lax.fori_loop(lo, hi, scores, jnp.full((1, ROWS), -1e30, F32))
        m = m * (SCALE * LOG2E)

        def sums(j, carried):
            l, r = carried
            d_t = lax.dot_general(kv[j, 1], g_i, nt, preferred_element_type=F32)
            d_buf[j] = d_t
            for half in range(2):
                rows = slice(half * BLK, (half + 1) * BLK)
                top = jnp.where(lane_seg == seg(2 * j + half), m, 1e30)
                e = jnp.exp2(s_buf[j, rows] * (SCALE * LOG2E) - top)
                s_buf[j, rows] = e
                l = l + jnp.sum(e, axis=0, keepdims=True)
                r = r + jnp.sum(e * d_t[rows], axis=0, keepdims=True)
            return l, r

        zero = jnp.zeros((1, ROWS), F32)
        l, r = lax.fori_loop(lo, hi, sums, (zero, zero))
        inv = 1.0 / l
        delta = r * inv

        def products(j, dq):
            p = s_buf[j] * inv
            ds = (p * (d_buf[j] - delta)).astype(BF16)
            dkv_acc[j, 1] += jnp.dot(p.astype(BF16), g_i, preferred_element_type=F32)
            dkv_acc[j, 0] += jnp.dot(ds, q_i, preferred_element_type=F32)
            return dq + lax.dot_general(ds, kv[j, 0], tn, preferred_element_type=F32)

        dq = lax.fori_loop(lo, hi, products, jnp.zeros((ROWS, HD), F32))
        dq_out[i] = (dq * SCALE).astype(BF16)
        return carry

    lax.fori_loop(0, 4, of_chunk, 0)
    dkv_out[:, 0] = (dkv_acc[:, 0] * SCALE).astype(BF16)
    dkv_out[:, 1] = dkv_acc[:, 1].astype(BF16)


def grads(sample_blocks, qg, kv):
    return pl.pallas_call(
        grads_kernel,
        out_shape=(
            jax.ShapeDtypeStruct((4, ROWS, HD), BF16),
            jax.ShapeDtypeStruct((16, 2, ROWS, HD), BF16),
        ),
        in_specs=[pl.BlockSpec(memory_space=pltpu.SMEM)] + [pl.BlockSpec(memory_space=pltpu.VMEM)] * 2,
        out_specs=(pl.BlockSpec(memory_space=pltpu.VMEM),) * 2,
        scratch_shapes=[
            pltpu.VMEM((16, ROWS, ROWS), F32),
            pltpu.VMEM((16, ROWS, ROWS), F32),
            pltpu.VMEM((16, 2, ROWS, HD), F32),
        ],
        compiler_params=pltpu.CompilerParams(vmem_limit_bytes=48 << 20),
        name="grads",
    )(sample_blocks, qg, kv)


def scatter_kernel(dq, dkv, dq_out, dk_out, dv_out, got_c, got_x, half_out, final, part,
                   c_send, c_recv, x_send, x_recv, y_send, y_recv, own):
    x, y, c = place()
    x_peer, c_peer = seq_id(1 - x, y, c), seq_id(x, y, 1 - c)
    y_of = lambda d: lax.rem(y + d, 4)
    meet([x_peer, c_peer] + [seq_id(x, y_of(d), c) for d in (1, 2, 3)])

    def chunk(xx, yy, cc):
        return xx * 8 + yy * 2 + cc

    def cols(ref, head):
        return ref.at[:, pl.ds(pl.multiple_of(head * HD, HD), HD)]

    def remote(src, dst, send, recv, device):
        return pltpu.make_async_remote_copy(
            src_ref=src, dst_ref=dst, send_sem=send, recv_sem=recv, device_id=device, device_id_type=MESH
        )

    sends = []

    def go(copy):
        copy.start()
        sends.append(copy)

    def arrived(dst, recv):
        remote(dst, dst, own.at[0], recv, x_peer).wait_recv()

    outs = (dq_out, dk_out, dv_out)
    order = (3, 1, 2, 0)
    for far in (1, 0):
        for d in order:
            xx = 1 - x if far else x
            go(remote(dkv.at[chunk(xx, y_of(d), 1 - c)], got_c.at[far, y_of(d)], c_send.at[far, d], c_recv.at[far, d], c_peer))
    for d in (1, 3, 2):
        go(remote(dq.at[y_of(d)], cols(dq_out, y), y_send.at[0, d], y_recv.at[0, d], seq_id(x, y_of(d), c)))
    own_q = pltpu.make_async_copy(dq.at[y], cols(dq_out, y), own.at[1])
    own_q.start()
    for d in order:
        yy = y_of(d)
        arrived(got_c.at[1, yy], c_recv.at[1, d])
        mine = dkv[chunk(1 - x, yy, c)].astype(F32) + got_c[1, yy].astype(F32)
        half_out[yy] = mine.astype(BF16)
        go(remote(half_out.at[yy], got_x.at[yy], x_send.at[d], x_recv.at[d], x_peer))
    for d in order:
        yy = y_of(d)
        arrived(got_c.at[0, yy], c_recv.at[0, d])
        part[yy] = dkv[chunk(x, yy, c)].astype(F32) + got_c[0, yy].astype(F32)
    own_kv = []
    for d in order:
        yy = y_of(d)
        arrived(got_x.at[yy], x_recv.at[d])
        final[yy] = (part[yy] + got_x[yy].astype(F32)).astype(BF16)
        for a in range(2):
            if d:
                go(remote(final.at[yy, a], cols(outs[a + 1], y), y_send.at[a + 1, d], y_recv.at[a + 1, d], seq_id(x, yy, c)))
            else:
                copy = pltpu.make_async_copy(final.at[yy, a], cols(outs[a + 1], y), own.at[2 + a])
                copy.start()
                own_kv.append(copy)
    for d in (3, 1, 2):
        for a in range(3):
            arrived(cols(outs[a], y_of(d)), y_recv.at[a, 4 - d])
    own_q.wait()
    for copy in own_kv:
        copy.wait()
    for copy in sends:
        copy.wait_send()


def scatter(dq, dkv):
    dma = pltpu.SemaphoreType.DMA
    out = jax.ShapeDtypeStruct((ROWS, 4 * HD), BF16)
    return pl.pallas_call(
        scatter_kernel,
        out_shape=(out,) * 3,
        in_specs=[pl.BlockSpec(memory_space=pltpu.VMEM)] * 2,
        out_specs=(pl.BlockSpec(memory_space=pltpu.VMEM),) * 3,
        scratch_shapes=[
            pltpu.VMEM((2, 4, 2, ROWS, HD), BF16),
            pltpu.VMEM((4, 2, ROWS, HD), BF16),
            pltpu.VMEM((4, 2, ROWS, HD), BF16),
            pltpu.VMEM((4, 2, ROWS, HD), BF16),
            pltpu.VMEM((4, 2, ROWS, HD), F32),
            dma((2, 4)), dma((2, 4)), dma((4,)), dma((4,)), dma((3, 4)), dma((3, 4)), dma((4,)),
        ],
        compiler_params=pltpu.CompilerParams(
            collective_id=1, has_side_effects=True, vmem_limit_bytes=32 << 20
        ),
        name="exchange_out",
    )(dq, dkv)


def local(query, key_rows, value_rows, out_grad, sample_blocks):
    qg, kv = gather(query, key_rows, value_rows, out_grad)
    dq, dkv = grads(sample_blocks, qg, kv)
    return scatter(dq, dkv)


def solution(mesh):
    spec = P("seq", "head")
    return jax.shard_map(
        local, mesh=mesh, in_specs=(spec, spec, spec, spec, P()), out_specs=(spec,) * 3, check_vma=False
    )
```

```python
import jax
import jax.numpy as jnp
from jax import lax
from jax.experimental import pallas as pl
from jax.experimental.pallas import tpu as pltpu
from jax.sharding import PartitionSpec as P

HD = 128
BLK = 128
ROWS = 256
QUERIES = 1024
MESH = pl.DeviceIdType.MESH
SCALE = HD**-0.5
EXP2_SCALE = SCALE * 1.4426950408889634
MASKED = -1e30
BF16 = jnp.bfloat16
F32 = jnp.float32
NT = (((1,), (1,)), ((), ()))


def place():
    s = lax.axis_index("seq")
    return lax.div(s, 8), lax.rem(lax.div(s, 2), 4), lax.rem(s, 2)


def seq_id(x, y, c):
    return {"seq": x * 8 + y * 2 + c}


def chunk(x, y, c):
    return x * 8 + y * 2 + c


def cols(ref, head):
    return ref.at[:, pl.ds(pl.multiple_of(head * HD, HD), HD)]


def rows(i):
    return pl.ds(pl.multiple_of(i * ROWS, ROWS), ROWS)


def kernel(
    blocks, q, k, v, g, dq_out, dk_out, dv_out,
    kv, qg, e_buf, d_buf, m_hist, stats, dq_acc, dq_low,
    to_core, got_core, keep, to_x, got_x, final, ends,
    y_send, y_recv, x_send, x_recv, c_send, c_recv, own,
    c2_send, c2_recv, x2_send, x2_recv, y2_send, y2_recv,
):
    x, y, c = place()
    x_peer, c_peer = seq_id(1 - x, y, c), seq_id(x, y, 1 - c)
    outs = (dq_out, dk_out, dv_out)

    def y_of(d):
        return lax.rem(y + d, 4)

    def remote(src, dst, send, recv, device):
        return pltpu.make_async_remote_copy(
            src_ref=src, dst_ref=dst, send_sem=send, recv_sem=recv, device_id=device, device_id_type=MESH
        )

    def arrived(dst, recv):
        remote(dst, dst, own.at[0], recv, x_peer).wait_recv()

    def sent(src, send):
        remote(src, src, send, own.at[0], x_peer).wait_send()

    here = chunk(x, y, c)
    own_copies = [
        pltpu.make_async_copy(cols(k, y), kv.at[here, 0], own.at[1]),
        pltpu.make_async_copy(cols(v, y), kv.at[here, 1], own.at[2]),
        pltpu.make_async_copy(cols(q, y), qg.at[0, rows(y)], own.at[3]),
        pltpu.make_async_copy(cols(g, y), qg.at[1, rows(y)], own.at[4]),
        pltpu.make_async_copy(blocks, ends, own.at[5]),
    ]
    for copy in own_copies:
        copy.start()

    peers = [x_peer, c_peer] + [seq_id(x, y_of(d), c) for d in (1, 2, 3)]
    barrier = pltpu.get_barrier_semaphore()
    for peer in peers:
        pl.semaphore_signal(barrier, inc=1, device_id=peer, device_id_type=MESH)
    pl.semaphore_wait(barrier, len(peers))

    sends = []

    def go(copy):
        copy.start()
        sends.append(copy)

    def y_keys(d):
        for a, ref in enumerate((k, v)):
            go(remote(cols(ref, y_of(d)), kv.at[here, a], y_send.at[a, d], y_recv.at[a, d], seq_id(x, y_of(d), c)))

    def y_queries(d):
        for a, ref in enumerate((q, g)):
            go(remote(cols(ref, y_of(d)), qg.at[a, rows(y)], y_send.at[a + 2, d], y_recv.at[a + 2, d], seq_id(x, y_of(d), c)))

    def onward(d):
        there = kv.at[chunk(x, y_of(d), c)]
        go(remote(there, there, x_send.at[d], x_recv.at[d], x_peer))
        go(remote(there, there, c_send.at[0, d], c_recv.at[0, d], c_peer))

    y_keys(1)
    y_keys(3)
    for copy in own_copies[:2]:
        copy.wait()
    onward(0)
    y_queries(1)
    y_queries(3)
    y_keys(2)
    y_queries(2)
    for d in (3, 1, 2):
        for a in range(2):
            arrived(kv.at[chunk(x, y_of(d), c), a], y_recv.at[a, 4 - d])
        onward(d)
    for copy in own_copies[2:]:
        copy.wait()
    for d in (3, 1, 2):
        for a in range(2):
            arrived(qg.at[a, rows(y_of(d))], y_recv.at[a + 2, 4 - d])
    for d in range(4):
        arrived(kv.at[chunk(x, y_of(d), 1 - c)], c_recv.at[0, d])

    end0 = ends[0]
    end1 = end0 + ends[1]
    lane = lax.broadcasted_iota(jnp.int32, (1, QUERIES), 1)
    lane_block = 16 * x + 2 * c + 4 * (lane >> 8) + ((lane >> 7) & 1)
    lane_seg = (lane_block >= end0).astype(jnp.int32) + (lane_block >= end1).astype(jnp.int32)
    stats[0] = jnp.full((1, QUERIES), MASKED, F32)
    stats[1] = jnp.zeros((1, QUERIES), F32)
    stats[2] = jnp.zeros((1, QUERIES), F32)

    def pass_a(t):
        for i in range(4):
            sl = slice(i * ROWS, (i + 1) * ROWS)
            s = lax.dot_general(kv[t, 0], qg[0, sl], NT, preferred_element_type=F32)
            d = lax.dot_general(kv[t, 1], qg[1, sl], NT, preferred_element_type=F32)
            m, l, r = stats[0, :, sl], stats[1, :, sl], stats[2, :, sl]
            halves = (slice(0, BLK), slice(BLK, ROWS))
            allowed = []
            new = m
            for h, half in enumerate(halves):
                key_block = 2 * t + h
                key_seg = (key_block >= end0).astype(jnp.int32) + (key_block >= end1).astype(jnp.int32)
                allowed.append(lane_seg[:, sl] == key_seg)
                top = jnp.max(s[half], axis=0, keepdims=True) * EXP2_SCALE
                new = jnp.maximum(new, jnp.where(allowed[h], top, MASKED))
            factor = jnp.exp2(m - new)
            l, r = l * factor, r * factor
            for h, half in enumerate(halves):
                top = jnp.where(allowed[h], new, -MASKED)
                e = jnp.exp2(s[half] * EXP2_SCALE - top)
                l = l + jnp.sum(e, axis=0, keepdims=True)
                r = r + jnp.sum(e * d[half], axis=0, keepdims=True)
                e_buf[t, half, sl] = e
            d_buf[t, :, sl] = d
            stats[0, :, sl], stats[1, :, sl], stats[2, :, sl] = new, l, r
            m_hist[t, :, sl] = new

    def a_near(n, carry):
        d = n + n // 2 - 2 * (n // 3)
        pass_a(chunk(x, y_of(d), c))
        far = kv.at[chunk(1 - x, y_of(d), c)]
        arrived(far, x_recv.at[d])
        remote(far, far, c_send.at[1, d], c_recv.at[1, d], c_peer).start()
        pass_a(chunk(x, y_of(d), 1 - c))
        return carry

    def a_far(n, carry):
        d = n + n // 2 - 2 * (n // 3)
        pass_a(chunk(1 - x, y_of(d), c))
        arrived(kv.at[chunk(1 - x, y_of(d), 1 - c)], c_recv.at[1, d])
        pass_a(chunk(1 - x, y_of(d), 1 - c))
        return carry

    lax.fori_loop(0, 4, a_near, 0)
    lax.fori_loop(0, 4, a_far, 0)

    inv = 1.0 / stats[1]
    stats[2] = stats[2] * inv
    stats[1] = inv
    dq_acc[...] = jnp.zeros_like(dq_acc)

    def pass_b(t, out):
        factor = jnp.exp2(m_hist[t] - stats[0]) * stats[1]
        p = e_buf[t] * factor
        ds = (p * (d_buf[t] - stats[2])).astype(BF16)
        out[1] = jnp.dot(p.astype(BF16), qg[1], preferred_element_type=F32)
        out[0] = jnp.dot(ds, qg[0], preferred_element_type=F32)
        dq_acc[...] += jnp.dot(kv[t, 0].T, ds, preferred_element_type=F32)

    def core_copy(far, d):
        return remote(to_core.at[far, d], got_core.at[far, d], c2_send.at[far, d], c2_recv.at[far, d], c_peer)

    def x_copy(d):
        return remote(to_x.at[d], got_x.at[d], x2_send.at[d], x2_recv.at[d], x_peer)

    def y_copy(a, d, src):
        return remote(src, cols(outs[a], y), y2_send.at[a, d], y2_recv.at[a, d], seq_id(x, y_of(d), c))

    def finish_far(d):
        arrived(got_core.at[0, d], c2_recv.at[0, d])
        to_x[d] = (keep[0, d] + got_core[0, d]).astype(BF16)
        x_copy(d).start()

    def sum_near(d):
        arrived(got_core.at[1, d], c2_recv.at[1, d])
        keep[1, d] = keep[1, d] + got_core[1, d]

    def finish_near(d):
        arrived(got_x.at[d], x2_recv.at[d])
        total = keep[1, d] + got_x[d].astype(F32)
        final[d, 0] = (total[0] * SCALE).astype(BF16)
        final[d, 1] = total[1].astype(BF16)

    def b_far(n, carry):
        d = lax.rem(n + 1, 4)
        pass_b(chunk(1 - x, y_of(d), 1 - c), to_core.at[0, d])
        core_copy(0, d).start()

        @pl.when(n > 0)
        def _():
            finish_far(n)

        pass_b(chunk(1 - x, y_of(d), c), keep.at[0, d])
        return carry

    def b_near(n, carry):
        d = lax.rem(n + 1, 4)
        pass_b(chunk(x, y_of(d), 1 - c), to_core.at[1, d])
        core_copy(1, d).start()

        @pl.when(n == 0)
        def _():
            finish_far(0)

        @pl.when(n > 0)
        def _():
            sum_near(n)

        @pl.when(n > 1)
        def _():
            finish_near(n - 1)
            for a in range(2):
                y_copy(a + 1, n - 1, final.at[n - 1, a]).start()

        pass_b(chunk(x, y_of(d), c), keep.at[1, d])
        return carry

    lax.fori_loop(0, 4, b_far, 0)
    lax.fori_loop(0, 4, b_near, 0)

    for i in range(4):
        dq_low[i * ROWS : (i + 1) * ROWS] = (dq_acc[:, i * ROWS : (i + 1) * ROWS].T * SCALE).astype(BF16)
    for d in (2, 1, 3):
        y_copy(0, d, dq_low.at[rows(y_of(d))]).start()
    last = [pltpu.make_async_copy(dq_low.at[rows(y)], cols(dq_out, y), own.at[1])]
    last[0].start()
    sum_near(0)
    finish_near(3)
    for a in range(2):
        y_copy(a + 1, 3, final.at[3, a]).start()
    finish_near(0)
    for a in range(2):
        copy = pltpu.make_async_copy(final.at[0, a], cols(outs[a + 1], y), own.at[2 + a])
        copy.start()
        last.append(copy)

    for d in (3, 2, 1):
        for a in range(3):
            arrived(cols(outs[a], y_of(d)), y2_recv.at[a, 4 - d])
    for copy in last:
        copy.wait()
    for copy in sends:
        copy.wait_send()
    for d in range(4):
        sent(kv.at[0], c_send.at[1, d])
        sent(to_core.at[0, d], c2_send.at[0, d])
        sent(to_core.at[1, d], c2_send.at[1, d])
        sent(to_x.at[d], x2_send.at[d])
    for d in (1, 2, 3):
        for a in range(3):
            sent(cols(outs[a], y), y2_send.at[a, d])


def local(query, key_rows, value_rows, out_grad, sample_blocks):
    dma = pltpu.SemaphoreType.DMA
    vmem = pltpu.VMEM
    out = jax.ShapeDtypeStruct((ROWS, 4 * HD), BF16)
    return pl.pallas_call(
        kernel,
        out_shape=(out,) * 3,
        in_specs=[pl.BlockSpec(memory_space=pl.ANY)] * 5,
        out_specs=(pl.BlockSpec(memory_space=vmem),) * 3,
        scratch_shapes=[
            vmem((16, 2, ROWS, HD), BF16),
            vmem((2, QUERIES, HD), BF16),
            vmem((16, ROWS, QUERIES), F32),
            vmem((16, ROWS, QUERIES), F32),
            vmem((16, 1, QUERIES), F32),
            vmem((3, 1, QUERIES), F32),
            vmem((HD, QUERIES), F32),
            vmem((QUERIES, HD), BF16),
            vmem((2, 4, 2, ROWS, HD), F32),
            vmem((2, 4, 2, ROWS, HD), F32),
            vmem((2, 4, 2, ROWS, HD), F32),
            vmem((4, 2, ROWS, HD), BF16),
            vmem((4, 2, ROWS, HD), BF16),
            vmem((4, 2, ROWS, HD), BF16),
            pltpu.SMEM((3,), jnp.int32),
            dma((4, 4)), dma((4, 4)), dma((4,)), dma((4,)), dma((2, 4)), dma((2, 4)), dma((6,)),
            dma((2, 4)), dma((2, 4)), dma((4,)), dma((4,)), dma((3, 4)), dma((3, 4)),
        ],
        compiler_params=pltpu.CompilerParams(
            collective_id=0, has_side_effects=True, vmem_limit_bytes=60 << 20
        ),
        name="attention_grads",
    )(sample_blocks, query, key_rows, value_rows, out_grad)


def solution(mesh):
    spec = P("seq", "head")
    return jax.shard_map(
        local, mesh=mesh, in_specs=(spec, spec, spec, spec, P()), out_specs=(spec,) * 3, check_vma=False
    )
```

```python
import jax
import jax.numpy as jnp
from jax import lax
from jax.experimental import pallas as pl
from jax.experimental.pallas import tpu as pltpu
from jax.sharding import PartitionSpec as P

HD = 128
BLK = 128
ROWS = 256
QUERIES = 1024
SLOT_OF = {0: 0, 1: 1, 3: 2, 2: 3}
MESH = pl.DeviceIdType.MESH
SCALE = HD**-0.5
EXP2_SCALE = SCALE * 1.4426950408889634
MASKED = -1e30
BF16 = jnp.bfloat16
F32 = jnp.float32
NT = (((1,), (1,)), ((), ()))


def place():
    s = lax.axis_index("seq")
    return lax.div(s, 8), lax.rem(lax.div(s, 2), 4), lax.rem(s, 2)


def seq_id(x, y, c):
    return {"seq": x * 8 + y * 2 + c}


def chunk(x, y, c):
    return x * 8 + y * 2 + c


def cols(ref, head):
    return ref.at[:, pl.ds(pl.multiple_of(head * HD, HD), HD)]


def rows(i):
    return pl.ds(pl.multiple_of(i * ROWS, ROWS), ROWS)


def kernel(
    blocks, q, k, v, g, dq_out, dk_out, dv_out,
    kv, qg, e_buf, d_buf, m_hist, stats, dq_acc, dq_low,
    to_core, got_core, keep, to_x, got_x, final, ends,
    y_send, y_recv, x_send, x_recv, c_send, c_recv, own,
    c2_send, c2_recv, x2_send, x2_recv, y2_send, y2_recv,
):
    x, y, c = place()
    x_peer, c_peer = seq_id(1 - x, y, c), seq_id(x, y, 1 - c)
    outs = (dq_out, dk_out, dv_out)

    def y_of(d):
        return lax.rem(y + d, 4)

    def remote(src, dst, send, recv, device):
        return pltpu.make_async_remote_copy(
            src_ref=src, dst_ref=dst, send_sem=send, recv_sem=recv, device_id=device, device_id_type=MESH
        )

    def arrived(dst, recv):
        remote(dst, dst, own.at[0], recv, x_peer).wait_recv()

    def sent(src, send):
        remote(src, src, send, own.at[0], x_peer).wait_send()

    here = chunk(x, y, c)
    own_copies = [
        pltpu.make_async_copy(cols(k, y), kv.at[here, 0], own.at[1]),
        pltpu.make_async_copy(cols(v, y), kv.at[here, 1], own.at[2]),
        pltpu.make_async_copy(cols(q, y), qg.at[0, rows(0)], own.at[3]),
        pltpu.make_async_copy(cols(g, y), qg.at[1, rows(0)], own.at[4]),
        pltpu.make_async_copy(blocks, ends, own.at[5]),
    ]
    for copy in own_copies:
        copy.start()

    peers = [x_peer, c_peer] + [seq_id(x, y_of(d), c) for d in (1, 2, 3)]
    barrier = pltpu.get_barrier_semaphore()
    for peer in peers:
        pl.semaphore_signal(barrier, inc=1, device_id=peer, device_id_type=MESH)
    pl.semaphore_wait(barrier, len(peers))

    sends = []

    def go(copy):
        copy.start()
        sends.append(copy)

    def y_keys(d):
        for a, ref in enumerate((k, v)):
            go(remote(cols(ref, y_of(d)), kv.at[here, a], y_send.at[a, d], y_recv.at[a, d], seq_id(x, y_of(d), c)))

    def y_queries(d):
        for a, ref in enumerate((q, g)):
            slot = qg.at[a, rows(SLOT_OF[4 - d])]
            go(remote(cols(ref, y_of(d)), slot, y_send.at[a + 2, d], y_recv.at[a + 2, d], seq_id(x, y_of(d), c)))

    def onward(d):
        there = kv.at[chunk(x, y_of(d), c)]
        remote(there, there, x_send.at[d], x_recv.at[d], x_peer).start()
        remote(there, there, c_send.at[0, d], c_recv.at[0, d], c_peer).start()

    y_keys(1)
    y_keys(3)
    for copy in own_copies[:2]:
        copy.wait()
    onward(0)
    y_queries(1)
    y_queries(3)
    y_keys(2)
    y_queries(2)
    def keys_arrived(d):
        for a in range(2):
            arrived(kv.at[chunk(x, y_of(d), c), a], y_recv.at[a, 4 - d])
        onward(d)

    def queries_arrived(d):
        for a in range(2):
            arrived(qg.at[a, rows(SLOT_OF[d])], y_recv.at[a + 2, 4 - d])

    def far_arrived(d):
        far = kv.at[chunk(1 - x, y_of(d), c)]
        arrived(far, x_recv.at[d])
        remote(far, far, c_send.at[1, d], c_recv.at[1, d], c_peer).start()

    for copy in own_copies[2:]:
        copy.wait()
    keys_arrived(3)
    keys_arrived(1)
    far_arrived(0)
    queries_arrived(3)
    queries_arrived(1)

    end0 = ends[0]
    end1 = end0 + ends[1]
    lane = lax.broadcasted_iota(jnp.int32, (1, QUERIES), 1)
    slot = lane >> 8
    lane_y = (y + jnp.where(slot == 3, 2, jnp.where(slot == 2, 3, slot))) & 3
    lane_block = 16 * x + 2 * c + 4 * lane_y + ((lane >> 7) & 1)
    lane_seg = (lane_block >= end0).astype(jnp.int32) + (lane_block >= end1).astype(jnp.int32)
    stats[0] = jnp.full((1, QUERIES), MASKED, F32)
    stats[1] = jnp.zeros((1, QUERIES), F32)
    stats[2] = jnp.zeros((1, QUERIES), F32)

    def pass_a(t, slots):
        for i in slots:
            sl = slice(i * ROWS, (i + 1) * ROWS)
            s = lax.dot_general(kv[t, 0], qg[0, sl], NT, preferred_element_type=F32)
            d = lax.dot_general(kv[t, 1], qg[1, sl], NT, preferred_element_type=F32)
            m, l, r = stats[0, :, sl], stats[1, :, sl], stats[2, :, sl]
            halves = (slice(0, BLK), slice(BLK, ROWS))
            allowed = []
            new = m
            for h, half in enumerate(halves):
                key_block = 2 * t + h
                key_seg = (key_block >= end0).astype(jnp.int32) + (key_block >= end1).astype(jnp.int32)
                allowed.append(lane_seg[:, sl] == key_seg)
                top = jnp.max(s[half], axis=0, keepdims=True) * EXP2_SCALE
                new = jnp.maximum(new, jnp.where(allowed[h], top, MASKED))
            factor = jnp.exp2(m - new)
            l, r = l * factor, r * factor
            for h, half in enumerate(halves):
                top = jnp.where(allowed[h], new, -MASKED)
                e = jnp.exp2(s[half] * EXP2_SCALE - top)
                l = l + jnp.sum(e, axis=0, keepdims=True)
                r = r + jnp.sum(e * d[half], axis=0, keepdims=True)
                e_buf[t, half, sl] = e
            d_buf[t, :, sl] = d
            stats[0, :, sl], stats[1, :, sl], stats[2, :, sl] = new, l, r
            m_hist[t, :, sl] = new

    def half_of(far):
        return x + far * (1 - 2 * x)

    def early(n):
        far = n // 3
        return far, (n + n // 2) * (1 - far)

    def a_first(n, carry):
        @pl.when(n == 2)
        def _():
            keys_arrived(2)

        far, d = early(n)
        pass_a(chunk(half_of(far), y_of(d), c), (0, 1, 2))
        peers_chunk = chunk(half_of(far), y_of(d), 1 - c)
        arrived(kv.at[peers_chunk], c_recv.at[far, d])
        pass_a(peers_chunk, (0, 1, 2))
        return carry

    def a_second(n, carry):
        far, d = early(n)
        pass_a(chunk(half_of(far), y_of(d), c), (3,))
        pass_a(chunk(half_of(far), y_of(d), 1 - c), (3,))
        return carry

    def a_third(n, carry):
        @pl.when(n == 2)
        def _():
            far_arrived(2)

        far, d = (n + 2) // 3, 2 + n - 3 * (n // 2)
        pass_a(chunk(half_of(far), y_of(d), c), (0, 1, 2, 3))
        peers_chunk = chunk(half_of(far), y_of(d), 1 - c)
        arrived(kv.at[peers_chunk], c_recv.at[far, d])
        pass_a(peers_chunk, (0, 1, 2, 3))
        return carry

    lax.fori_loop(0, 4, a_first, 0)
    far_arrived(3)
    queries_arrived(2)
    lax.fori_loop(0, 4, a_second, 0)
    far_arrived(1)
    lax.fori_loop(0, 4, a_third, 0)

    inv = 1.0 / stats[1]
    stats[2] = stats[2] * inv
    stats[1] = inv
    dq_acc[...] = jnp.zeros_like(dq_acc)

    def pass_b(t, out):
        factor = jnp.exp2(m_hist[t] - stats[0]) * stats[1]
        p = e_buf[t] * factor
        ds = (p * (d_buf[t] - stats[2])).astype(BF16)
        out[1] = jnp.dot(p.astype(BF16), qg[1], preferred_element_type=F32)
        out[0] = jnp.dot(ds, qg[0], preferred_element_type=F32)
        dq_acc[...] += jnp.dot(kv[t, 0].T, ds, preferred_element_type=F32)

    def core_copy(far, d):
        return remote(to_core.at[far, d], got_core.at[far, d], c2_send.at[far, d], c2_recv.at[far, d], c_peer)

    def x_copy(d):
        return remote(to_x.at[d], got_x.at[d], x2_send.at[d], x2_recv.at[d], x_peer)

    def y_copy(a, d, src):
        return remote(src, cols(outs[a], y), y2_send.at[a, d], y2_recv.at[a, d], seq_id(x, y_of(d), c))

    def finish_far(d):
        arrived(got_core.at[0, d], c2_recv.at[0, d])
        to_x[d] = (keep[0, d] + got_core[0, d]).astype(BF16)
        x_copy(d).start()

    def sum_near(d):
        arrived(got_core.at[1, d], c2_recv.at[1, d])
        keep[1, d] = keep[1, d] + got_core[1, d]

    def finish_near(d):
        arrived(got_x.at[d], x2_recv.at[d])
        total = keep[1, d] + got_x[d].astype(F32)
        final[d, 0] = (total[0] * SCALE).astype(BF16)
        final[d, 1] = total[1].astype(BF16)

    def b_far(n, carry):
        d = lax.rem(n + 1, 4)
        pass_b(chunk(1 - x, y_of(d), 1 - c), to_core.at[0, d])
        core_copy(0, d).start()

        @pl.when(n > 0)
        def _():
            finish_far(n)

        pass_b(chunk(1 - x, y_of(d), c), keep.at[0, d])
        return carry

    def b_near(n, carry):
        d = lax.rem(n + 1, 4)
        pass_b(chunk(x, y_of(d), 1 - c), to_core.at[1, d])
        core_copy(1, d).start()

        @pl.when(n == 0)
        def _():
            finish_far(0)

        @pl.when(n > 0)
        def _():
            sum_near(n)

        @pl.when(n > 1)
        def _():
            finish_near(n - 1)
            for a in range(2):
                y_copy(a + 1, n - 1, final.at[n - 1, a]).start()

        pass_b(chunk(x, y_of(d), c), keep.at[1, d])
        return carry

    lax.fori_loop(0, 4, b_far, 0)
    lax.fori_loop(0, 4, b_near, 0)

    for i in range(4):
        dq_low[i * ROWS : (i + 1) * ROWS] = (dq_acc[:, i * ROWS : (i + 1) * ROWS].T * SCALE).astype(BF16)
    for d in (2, 1, 3):
        y_copy(0, d, dq_low.at[rows(SLOT_OF[d])]).start()
    own_cols = pl.ds(pl.multiple_of(y * HD, HD), HD)
    dq_out[:, own_cols] = dq_low[:ROWS]
    sum_near(0)
    finish_near(3)
    for a in range(2):
        y_copy(a + 1, 3, final.at[3, a]).start()
    finish_near(0)
    for a in range(2):
        outs[a + 1][:, own_cols] = final[0, a]

    for d in (3, 2, 1):
        for a in range(3):
            arrived(cols(outs[a], y_of(d)), y2_recv.at[a, 4 - d])
    for copy in sends:
        copy.wait_send()
    for d in range(4):
        sent(kv.at[0], x_send.at[d])
        sent(kv.at[0], c_send.at[0, d])
        sent(kv.at[0], c_send.at[1, d])
        sent(to_core.at[0, d], c2_send.at[0, d])
        sent(to_core.at[1, d], c2_send.at[1, d])
        sent(to_x.at[d], x2_send.at[d])
    for d in (1, 2, 3):
        for a in range(3):
            sent(cols(outs[a], y), y2_send.at[a, d])


def store_kernel(dq, dk, dv, dq_out, dk_out, dv_out, done):
    copies = [
        pltpu.make_async_copy(src, dst, done.at[i])
        for i, (src, dst) in enumerate(((dq, dq_out), (dk, dk_out), (dv, dv_out)))
    ]
    for copy in copies:
        copy.start()
    for copy in copies:
        copy.wait()


def local(query, key_rows, value_rows, out_grad, sample_blocks):
    dma = pltpu.SemaphoreType.DMA
    vmem = pltpu.VMEM
    out = jax.ShapeDtypeStruct((ROWS, 4 * HD), BF16)
    grads = pl.pallas_call(
        kernel,
        out_shape=(out,) * 3,
        in_specs=[pl.BlockSpec(memory_space=pl.ANY)] * 5,
        out_specs=(pl.BlockSpec(memory_space=vmem),) * 3,
        scratch_shapes=[
            vmem((16, 2, ROWS, HD), BF16),
            vmem((2, QUERIES, HD), BF16),
            vmem((16, ROWS, QUERIES), F32),
            vmem((16, ROWS, QUERIES), F32),
            vmem((16, 1, QUERIES), F32),
            vmem((3, 1, QUERIES), F32),
            vmem((HD, QUERIES), F32),
            vmem((QUERIES, HD), BF16),
            vmem((2, 4, 2, ROWS, HD), F32),
            vmem((2, 4, 2, ROWS, HD), F32),
            vmem((2, 4, 2, ROWS, HD), F32),
            vmem((4, 2, ROWS, HD), BF16),
            vmem((4, 2, ROWS, HD), BF16),
            vmem((4, 2, ROWS, HD), BF16),
            pltpu.SMEM((3,), jnp.int32),
            dma((4, 4)), dma((4, 4)), dma((4,)), dma((4,)), dma((2, 4)), dma((2, 4)), dma((6,)),
            dma((2, 4)), dma((2, 4)), dma((4,)), dma((4,)), dma((3, 4)), dma((3, 4)),
        ],
        compiler_params=pltpu.CompilerParams(
            collective_id=0, has_side_effects=True, vmem_limit_bytes=60 << 20
        ),
        name="attention_grads",
    )(sample_blocks, query, key_rows, value_rows, out_grad)
    return pl.pallas_call(
        store_kernel,
        out_shape=(out,) * 3,
        in_specs=[pl.BlockSpec(memory_space=vmem)] * 3,
        out_specs=(pl.BlockSpec(memory_space=pl.ANY),) * 3,
        scratch_shapes=[dma((3,))],
        name="store",
    )(*grads)


def solution(mesh):
    spec = P("seq", "head")
    return jax.shard_map(
        local, mesh=mesh, in_specs=(spec, spec, spec, spec, P()), out_specs=(spec,) * 3, check_vma=False
    )
```

```python
import jax
import jax.numpy as jnp
from jax import lax
from jax.experimental import pallas as pl
from jax.experimental.pallas import tpu as pltpu
from jax.sharding import PartitionSpec as P

HD = 128
BLK = 128
ROWS = 256
QUERIES = 1024
SLOT_OF = {0: 0, 1: 1, 3: 2, 2: 3}
MESH = pl.DeviceIdType.MESH
SCALE = HD**-0.5
EXP2_SCALE = SCALE * 1.4426950408889634
MASKED = -1e30
BF16 = jnp.bfloat16
F32 = jnp.float32
NT = (((1,), (1,)), ((), ()))


def place():
    s = lax.axis_index("seq")
    return lax.div(s, 8), lax.rem(lax.div(s, 2), 4), lax.rem(s, 2)


def seq_id(x, y, c):
    return {"seq": x * 8 + y * 2 + c}


def chunk(x, y, c):
    return x * 8 + y * 2 + c


def cols(ref, head):
    return ref.at[:, pl.ds(pl.multiple_of(head * HD, HD), HD)]


def rows(i):
    return pl.ds(pl.multiple_of(i * ROWS, ROWS), ROWS)


def kernel(
    blocks, q, k, v, g, dq_out, dk_out, dv_out,
    kv, qg, e_buf, d_buf, m_hist, stats, dq_acc, dq_low,
    to_core, got_core, keep, to_x, got_x, final, ends,
    y_send, y_recv, x_send, x_recv, c_send, c_recv, own,
    c2_send, c2_recv, x2_send, x2_recv, y2_send, y2_recv,
):
    x, y, c = place()
    x_peer, c_peer = seq_id(1 - x, y, c), seq_id(x, y, 1 - c)
    outs = (dq_out, dk_out, dv_out)

    def y_of(d):
        return lax.rem(y + d, 4)

    def remote(src, dst, send, recv, device):
        return pltpu.make_async_remote_copy(
            src_ref=src, dst_ref=dst, send_sem=send, recv_sem=recv, device_id=device, device_id_type=MESH
        )

    def arrived(dst, recv):
        remote(dst, dst, own.at[0], recv, x_peer).wait_recv()

    def sent(src, send):
        remote(src, src, send, own.at[0], x_peer).wait_send()

    here = chunk(x, y, c)
    own_copies = [
        pltpu.make_async_copy(cols(k, y), kv.at[here, 0], own.at[1]),
        pltpu.make_async_copy(cols(v, y), kv.at[here, 1], own.at[2]),
        pltpu.make_async_copy(cols(q, y), qg.at[0, rows(0)], own.at[3]),
        pltpu.make_async_copy(cols(g, y), qg.at[1, rows(0)], own.at[4]),
        pltpu.make_async_copy(blocks, ends, own.at[5]),
    ]
    for copy in own_copies:
        copy.start()

    peers = [x_peer, c_peer] + [seq_id(x, y_of(d), c) for d in (1, 2, 3)]
    barrier = pltpu.get_barrier_semaphore()
    for peer in peers:
        pl.semaphore_signal(barrier, inc=1, device_id=peer, device_id_type=MESH)
    pl.semaphore_wait(barrier, len(peers))

    sends = []

    def go(copy):
        copy.start()
        sends.append(copy)

    def y_keys(a, d):
        src = cols((k, v)[a], y_of(d))
        go(remote(src, kv.at[here, a], y_send.at[a, d], y_recv.at[a, d], seq_id(x, y_of(d), c)))

    def y_queries(d):
        for a, ref in enumerate((q, g)):
            slot = qg.at[a, rows(SLOT_OF[4 - d])]
            go(remote(cols(ref, y_of(d)), slot, y_send.at[a + 2, d], y_recv.at[a + 2, d], seq_id(x, y_of(d), c)))

    def onward(a, d):
        there = kv.at[chunk(x, y_of(d), c), a]
        remote(there, there, x_send.at[a, d], x_recv.at[a, d], x_peer).start()
        remote(there, there, c_send.at[0, a, d], c_recv.at[0, a, d], c_peer).start()

    for a in range(2):
        for d in (1, 3):
            y_keys(a, d)
    for a in range(2):
        own_copies[a].wait()
        onward(a, 0)
    y_queries(1)
    y_queries(3)
    for a in range(2):
        y_keys(a, 2)
    y_queries(2)
    def half_of(far):
        return x + far * (1 - 2 * x)

    def keys_arrived(a, d):
        arrived(kv.at[chunk(x, y_of(d), c), a], y_recv.at[a, 4 - d])
        onward(a, d)

    def queries_arrived(d):
        for a in range(2):
            arrived(qg.at[a, rows(SLOT_OF[d])], y_recv.at[a + 2, 4 - d])

    def far_arrived(d):
        for a in range(2):
            far = kv.at[chunk(1 - x, y_of(d), c), a]
            arrived(far, x_recv.at[a, d])
            remote(far, far, c_send.at[1, a, d], c_recv.at[1, a, d], c_peer).start()

    def core_arrived(far, d):
        t = chunk(half_of(far), y_of(d), 1 - c)
        for a in range(2):
            arrived(kv.at[t, a], c_recv.at[far, a, d])
        return t

    for copy in own_copies[2:]:
        copy.wait()
    for a in range(2):
        for d in (3, 1):
            keys_arrived(a, d)
    far_arrived(0)
    queries_arrived(3)
    queries_arrived(1)

    end0 = ends[0]
    end1 = end0 + ends[1]
    lane = lax.broadcasted_iota(jnp.int32, (1, QUERIES), 1)
    slot = lane >> 8
    lane_y = (y + jnp.where(slot == 3, 2, jnp.where(slot == 2, 3, slot))) & 3
    lane_block = 16 * x + 2 * c + 4 * lane_y + ((lane >> 7) & 1)
    lane_seg = (lane_block >= end0).astype(jnp.int32) + (lane_block >= end1).astype(jnp.int32)
    stats[0] = jnp.full((1, QUERIES), MASKED, F32)
    stats[1] = jnp.zeros((1, QUERIES), F32)
    stats[2] = jnp.zeros((1, QUERIES), F32)

    def pass_a(t, slots):
        for i in slots:
            sl = slice(i * ROWS, (i + 1) * ROWS)
            s = lax.dot_general(kv[t, 0], qg[0, sl], NT, preferred_element_type=F32)
            d = lax.dot_general(kv[t, 1], qg[1, sl], NT, preferred_element_type=F32)
            m, l, r = stats[0, :, sl], stats[1, :, sl], stats[2, :, sl]
            halves = (slice(0, BLK), slice(BLK, ROWS))
            allowed = []
            new = m
            for h, half in enumerate(halves):
                key_block = 2 * t + h
                key_seg = (key_block >= end0).astype(jnp.int32) + (key_block >= end1).astype(jnp.int32)
                allowed.append(lane_seg[:, sl] == key_seg)
                top = jnp.max(s[half], axis=0, keepdims=True) * EXP2_SCALE
                new = jnp.maximum(new, jnp.where(allowed[h], top, MASKED))
            factor = jnp.exp2(m - new)
            l, r = l * factor, r * factor
            for h, half in enumerate(halves):
                top = jnp.where(allowed[h], new, -MASKED)
                e = jnp.exp2(s[half] * EXP2_SCALE - top)
                l = l + jnp.sum(e, axis=0, keepdims=True)
                r = r + jnp.sum(e * d[half], axis=0, keepdims=True)
                e_buf[t, half, sl] = e
            d_buf[t, :, sl] = d
            stats[0, :, sl], stats[1, :, sl], stats[2, :, sl] = new, l, r
            m_hist[t, :, sl] = new

    def early(n):
        far = n // 3
        return far, (n + n // 2) * (1 - far)

    def a_first(n, carry):
        @pl.when(n == 2)
        def _():
            for a in range(2):
                keys_arrived(a, 2)

        far, d = early(n)
        pass_a(chunk(half_of(far), y_of(d), c), (0, 1, 2))
        pass_a(core_arrived(far, d), (0, 1, 2))
        return carry

    def a_second(n, carry):
        far, d = early(n)
        pass_a(chunk(half_of(far), y_of(d), c), (3,))
        pass_a(chunk(half_of(far), y_of(d), 1 - c), (3,))
        return carry

    def a_third(n, carry):
        @pl.when(n == 2)
        def _():
            far_arrived(2)

        far, d = (n + 2) // 3, 2 + n - 3 * (n // 2)
        pass_a(chunk(half_of(far), y_of(d), c), (0, 1, 2, 3))
        pass_a(core_arrived(far, d), (0, 1, 2, 3))
        return carry

    lax.fori_loop(0, 4, a_first, 0)
    far_arrived(3)
    queries_arrived(2)
    lax.fori_loop(0, 4, a_second, 0)
    far_arrived(1)
    lax.fori_loop(0, 4, a_third, 0)

    inv = 1.0 / stats[1]
    stats[2] = stats[2] * inv
    stats[1] = inv
    dq_acc[...] = jnp.zeros_like(dq_acc)

    def pass_b(t, out):
        factor = jnp.exp2(m_hist[t] - stats[0]) * stats[1]
        p = e_buf[t] * factor
        ds = (p * (d_buf[t] - stats[2])).astype(BF16)
        out[1] = jnp.dot(p.astype(BF16), qg[1], preferred_element_type=F32)
        out[0] = jnp.dot(ds, qg[0], preferred_element_type=F32)
        dq_acc[...] += jnp.dot(kv[t, 0].T, ds, preferred_element_type=F32)

    def core_copy(far, d):
        return remote(to_core.at[far, d], got_core.at[far, d], c2_send.at[far, d], c2_recv.at[far, d], c_peer)

    def x_copy(a, d):
        return remote(to_x.at[d, a], got_x.at[d, a], x2_send.at[a, d], x2_recv.at[a, d], x_peer)

    def y_copy(a, d, src):
        return remote(src, cols(outs[a], y), y2_send.at[a, d], y2_recv.at[a, d], seq_id(x, y_of(d), c))

    def sum_far(d):
        arrived(got_core.at[0, d], c2_recv.at[0, d])
        to_x[d] = (keep[0, d] + got_core[0, d]).astype(BF16)

    def sum_near(d):
        arrived(got_core.at[1, d], c2_recv.at[1, d])
        keep[1, d] = keep[1, d] + got_core[1, d]

    def final_sum(a, d):
        arrived(got_x.at[d, a], x2_recv.at[a, d])
        total = keep[1, d, a] + got_x[d, a].astype(F32)
        return (total if a else total * SCALE).astype(BF16)

    def finish(a, d):
        final[d, a] = final_sum(a, d)
        y_copy(a + 1, d, final.at[d, a]).start()

    def distance(n):
        back = 3 - n
        return back + back // 2 - 2 * (back // 3)

    def b_far(n, carry):
        d = distance(n)
        pass_b(chunk(1 - x, y_of(d), 1 - c), to_core.at[0, d])
        core_copy(0, d).start()

        @pl.when(n == 1)
        def _():
            sum_far(2)
            for a in range(2):
                x_copy(a, 2).start()

        @pl.when(n == 2)
        def _():
            sum_far(3)
            x_copy(0, 3).start()

        @pl.when(n == 3)
        def _():
            sum_far(1)
            x_copy(0, 1).start()
            x_copy(1, 3).start()
            x_copy(1, 1).start()

        pass_b(chunk(1 - x, y_of(d), c), keep.at[0, d])
        return carry

    def b_near(n, carry):
        d = distance(n)
        pass_b(chunk(x, y_of(d), 1 - c), to_core.at[1, d])
        core_copy(1, d).start()

        @pl.when(n == 0)
        def _():
            sum_far(0)
            for a in range(2):
                x_copy(a, 0).start()

        @pl.when(n == 1)
        def _():
            sum_near(2)

        @pl.when(n == 2)
        def _():
            sum_near(3)
            finish(0, 2)

        @pl.when(n == 3)
        def _():
            sum_near(1)
            finish(1, 2)

        pass_b(chunk(x, y_of(d), c), keep.at[1, d])
        return carry

    lax.fori_loop(0, 4, b_far, 0)
    lax.fori_loop(0, 4, b_near, 0)

    for i in range(4):
        dq_low[i * ROWS : (i + 1) * ROWS] = (dq_acc[:, i * ROWS : (i + 1) * ROWS].T * SCALE).astype(BF16)
    for d in (2, 1, 3):
        y_copy(0, d, dq_low.at[rows(SLOT_OF[d])]).start()
    own_cols = pl.ds(pl.multiple_of(y * HD, HD), HD)
    dq_out[:, own_cols] = dq_low[:ROWS]
    sum_near(0)
    for a in range(2):
        finish(a, 3)
        finish(a, 1)
    for a in range(2):
        outs[a + 1][:, own_cols] = final_sum(a, 0)

    for d in (3, 2, 1):
        for a in range(3):
            arrived(cols(outs[a], y_of(d)), y2_recv.at[a, 4 - d])
    for copy in sends:
        copy.wait_send()
    for d in range(4):
        for a in range(2):
            sent(kv.at[0, 0], x_send.at[a, d])
            sent(kv.at[0, 0], c_send.at[0, a, d])
            sent(kv.at[0, 0], c_send.at[1, a, d])
            sent(to_x.at[d, a], x2_send.at[a, d])
        sent(to_core.at[0, d], c2_send.at[0, d])
        sent(to_core.at[1, d], c2_send.at[1, d])
    for d in (1, 2, 3):
        for a in range(3):
            sent(cols(outs[a], y), y2_send.at[a, d])


def store_kernel(dq, dk, dv, dq_out, dk_out, dv_out, done):
    copies = [
        pltpu.make_async_copy(src, dst, done.at[i])
        for i, (src, dst) in enumerate(((dq, dq_out), (dk, dk_out), (dv, dv_out)))
    ]
    for copy in copies:
        copy.start()
    for copy in copies:
        copy.wait()


def local(query, key_rows, value_rows, out_grad, sample_blocks):
    dma = pltpu.SemaphoreType.DMA
    vmem = pltpu.VMEM
    out = jax.ShapeDtypeStruct((ROWS, 4 * HD), BF16)
    grads = pl.pallas_call(
        kernel,
        out_shape=(out,) * 3,
        in_specs=[pl.BlockSpec(memory_space=pl.ANY)] * 5,
        out_specs=(pl.BlockSpec(memory_space=vmem),) * 3,
        scratch_shapes=[
            vmem((16, 2, ROWS, HD), BF16),
            vmem((2, QUERIES, HD), BF16),
            vmem((16, ROWS, QUERIES), F32),
            vmem((16, ROWS, QUERIES), F32),
            vmem((16, 1, QUERIES), F32),
            vmem((3, 1, QUERIES), F32),
            vmem((HD, QUERIES), F32),
            vmem((QUERIES, HD), BF16),
            vmem((2, 4, 2, ROWS, HD), F32),
            vmem((2, 4, 2, ROWS, HD), F32),
            vmem((2, 4, 2, ROWS, HD), F32),
            vmem((4, 2, ROWS, HD), BF16),
            vmem((4, 2, ROWS, HD), BF16),
            vmem((4, 2, ROWS, HD), BF16),
            pltpu.SMEM((3,), jnp.int32),
            dma((4, 4)), dma((4, 4)), dma((2, 4)), dma((2, 4)), dma((2, 2, 4)), dma((2, 2, 4)), dma((6,)),
            dma((2, 4)), dma((2, 4)), dma((2, 4)), dma((2, 4)), dma((3, 4)), dma((3, 4)),
        ],
        compiler_params=pltpu.CompilerParams(
            collective_id=0, has_side_effects=True, vmem_limit_bytes=60 << 20
        ),
        name="attention_grads",
    )(sample_blocks, query, key_rows, value_rows, out_grad)
    return pl.pallas_call(
        store_kernel,
        out_shape=(out,) * 3,
        in_specs=[pl.BlockSpec(memory_space=vmem)] * 3,
        out_specs=(pl.BlockSpec(memory_space=pl.ANY),) * 3,
        scratch_shapes=[dma((3,))],
        name="store",
    )(*grads)


def solution(mesh):
    spec = P("seq", "head")
    return jax.shard_map(
        local, mesh=mesh, in_specs=(spec, spec, spec, spec, P()), out_specs=(spec,) * 3, check_vma=False
    )
```

```python
import jax
import jax.numpy as jnp
from jax import lax
from jax.experimental import pallas as pl
from jax.experimental.pallas import tpu as pltpu
from jax.sharding import PartitionSpec as P

HD = 128
BLK = 128
ROWS = 256
QUERIES = 1024
SLOT_OF = {0: 0, 1: 1, 3: 2, 2: 3}
MESH = pl.DeviceIdType.MESH
SCALE = HD**-0.5
EXP2_SCALE = SCALE * 1.4426950408889634
MASKED = -1e30
BF16 = jnp.bfloat16
F32 = jnp.float32
NT = (((1,), (1,)), ((), ()))


def place():
    s = lax.axis_index("seq")
    return lax.div(s, 8), lax.rem(lax.div(s, 2), 4), lax.rem(s, 2)


def seq_id(x, y, c):
    return {"seq": x * 8 + y * 2 + c}


def chunk(x, y, c):
    return x * 8 + y * 2 + c


def cols(ref, head):
    return ref.at[:, pl.ds(pl.multiple_of(head * HD, HD), HD)]


def rows(i):
    return pl.ds(pl.multiple_of(i * ROWS, ROWS), ROWS)


def kernel(
    blocks, q, k, v, g, dq_out, dk_out, dv_out,
    kv, qg, e_buf, d_buf, m_hist, stats, dq_acc, dq_low,
    to_core, got_core, keep, to_x, got_x, final, ends,
    y_send, y_recv, x_send, x_recv, c_send, c_recv, own,
    c2_send, c2_recv, x2_send, x2_recv, y2_send, y2_recv,
):
    x, y, c = place()
    x_peer, c_peer = seq_id(1 - x, y, c), seq_id(x, y, 1 - c)
    outs = (dq_out, dk_out, dv_out)

    def y_of(d):
        return lax.rem(y + d, 4)

    def remote(src, dst, send, recv, device):
        return pltpu.make_async_remote_copy(
            src_ref=src, dst_ref=dst, send_sem=send, recv_sem=recv, device_id=device, device_id_type=MESH
        )

    def arrived(dst, recv):
        remote(dst, dst, own.at[0], recv, x_peer).wait_recv()

    def sent(src, send):
        remote(src, src, send, own.at[0], x_peer).wait_send()

    peers = [x_peer, c_peer] + [seq_id(x, y_of(d), c) for d in (1, 2, 3)]
    barrier = pltpu.get_barrier_semaphore()
    for peer in peers:
        pl.semaphore_signal(barrier, inc=1, device_id=peer, device_id_type=MESH)

    here = chunk(x, y, c)
    own_copies = [
        pltpu.make_async_copy(cols(k, y), kv.at[here, 0], own.at[1]),
        pltpu.make_async_copy(cols(v, y), kv.at[here, 1], own.at[2]),
        pltpu.make_async_copy(cols(q, y), qg.at[0, rows(0)], own.at[3]),
        pltpu.make_async_copy(cols(g, y), qg.at[1, rows(0)], own.at[4]),
        pltpu.make_async_copy(blocks, ends, own.at[5]),
    ]
    for copy in own_copies:
        copy.start()

    pl.semaphore_wait(barrier, len(peers))

    sends = []

    def go(copy):
        copy.start()
        sends.append(copy)

    def y_keys(a, d):
        src = cols((k, v)[a], y_of(d))
        go(remote(src, kv.at[here, a], y_send.at[a, d], y_recv.at[a, d], seq_id(x, y_of(d), c)))

    def y_queries(d):
        for a, ref in enumerate((q, g)):
            slot = qg.at[a, rows(SLOT_OF[4 - d])]
            go(remote(cols(ref, y_of(d)), slot, y_send.at[a + 2, d], y_recv.at[a + 2, d], seq_id(x, y_of(d), c)))

    def onward(a, d):
        there = kv.at[chunk(x, y_of(d), c), a]
        remote(there, there, x_send.at[a, d], x_recv.at[a, d], x_peer).start()
        remote(there, there, c_send.at[0, a, d], c_recv.at[0, a, d], c_peer).start()

    for a in range(2):
        for d in (1, 3):
            y_keys(a, d)
    for a in range(2):
        own_copies[a].wait()
        onward(a, 0)
    y_queries(1)
    y_queries(3)
    for a in range(2):
        y_keys(a, 2)
    y_queries(2)
    def half_of(far):
        return x + far * (1 - 2 * x)

    def keys_arrived(a, d):
        arrived(kv.at[chunk(x, y_of(d), c), a], y_recv.at[a, 4 - d])
        onward(a, d)

    def queries_arrived(d):
        for a in range(2):
            arrived(qg.at[a, rows(SLOT_OF[d])], y_recv.at[a + 2, 4 - d])

    def far_arrived(d):
        for a in range(2):
            far = kv.at[chunk(1 - x, y_of(d), c), a]
            arrived(far, x_recv.at[a, d])
            remote(far, far, c_send.at[1, a, d], c_recv.at[1, a, d], c_peer).start()

    def core_arrived(far, d):
        t = chunk(half_of(far), y_of(d), 1 - c)
        for a in range(2):
            arrived(kv.at[t, a], c_recv.at[far, a, d])
        return t

    for copy in own_copies[2:]:
        copy.wait()
    for a in range(2):
        for d in (3, 1):
            keys_arrived(a, d)
    far_arrived(0)

    end0 = ends[0]
    end1 = end0 + ends[1]
    lane = lax.broadcasted_iota(jnp.int32, (1, QUERIES), 1)
    slot = lane >> 8
    lane_y = (y + jnp.where(slot == 3, 2, jnp.where(slot == 2, 3, slot))) & 3
    lane_block = 16 * x + 2 * c + 4 * lane_y + ((lane >> 7) & 1)
    lane_seg = (lane_block >= end0).astype(jnp.int32) + (lane_block >= end1).astype(jnp.int32)
    stats[0] = jnp.full((1, QUERIES), MASKED, F32)
    stats[1] = jnp.zeros((1, QUERIES), F32)
    stats[2] = jnp.zeros((1, QUERIES), F32)

    def pass_a(t, slots):
        for i in slots:
            sl = slice(i * ROWS, (i + 1) * ROWS)
            s = lax.dot_general(kv[t, 0], qg[0, sl], NT, preferred_element_type=F32)
            d = lax.dot_general(kv[t, 1], qg[1, sl], NT, preferred_element_type=F32)
            m, l, r = stats[0, :, sl], stats[1, :, sl], stats[2, :, sl]
            halves = (slice(0, BLK), slice(BLK, ROWS))
            allowed = []
            new = m
            for h, half in enumerate(halves):
                key_block = 2 * t + h
                key_seg = (key_block >= end0).astype(jnp.int32) + (key_block >= end1).astype(jnp.int32)
                allowed.append(lane_seg[:, sl] == key_seg)
                top = jnp.max(s[half], axis=0, keepdims=True) * EXP2_SCALE
                new = jnp.maximum(new, jnp.where(allowed[h], top, MASKED))
            factor = jnp.exp2(m - new)
            l, r = l * factor, r * factor
            for h, half in enumerate(halves):
                top = jnp.where(allowed[h], new, -MASKED)
                e = jnp.exp2(s[half] * EXP2_SCALE - top)
                l = l + jnp.sum(e, axis=0, keepdims=True)
                r = r + jnp.sum(e * d[half], axis=0, keepdims=True)
                e_buf[t, half, sl] = e
            d_buf[t, :, sl] = d
            stats[0, :, sl], stats[1, :, sl], stats[2, :, sl] = new, l, r
            m_hist[t, :, sl] = new

    def early(n):
        far = n // 3
        return far, (n + n // 2) * (1 - far)

    def a_own(n, carry):
        far, d = early(n)
        pass_a(chunk(half_of(far), y_of(d), c), (0,))
        pass_a(core_arrived(far, d), (0,))
        return carry

    def a_first(n, carry):
        @pl.when(n == 3)
        def _():
            for a in range(2):
                keys_arrived(a, 2)

        far, d = early(n)
        pass_a(chunk(half_of(far), y_of(d), c), (1, 2))
        pass_a(chunk(half_of(far), y_of(d), 1 - c), (1, 2))
        return carry

    def a_second(n, carry):
        for item in (2 * n, 2 * n + 1):
            far, d = early(item)
            for core in (c, 1 - c):
                pass_a(chunk(half_of(far), y_of(d), core), (3,))
        return carry

    def a_third(n, carry):
        @pl.when(n == 2)
        def _():
            far_arrived(2)

        far, d = (n + 2) // 3, 2 + n - 3 * (n // 2)
        pass_a(chunk(half_of(far), y_of(d), c), (0, 1, 2, 3))
        pass_a(core_arrived(far, d), (0, 1, 2, 3))
        return carry

    lax.fori_loop(0, 4, a_own, 0)
    queries_arrived(3)
    queries_arrived(1)
    lax.fori_loop(0, 4, a_first, 0)
    far_arrived(3)
    queries_arrived(2)
    lax.fori_loop(0, 2, a_second, 0)
    far_arrived(1)
    lax.fori_loop(0, 4, a_third, 0)

    inv = 1.0 / stats[1]
    stats[2] = stats[2] * inv
    stats[1] = inv
    dq_acc[...] = jnp.zeros_like(dq_acc)

    def pass_b(t, out):
        factor = jnp.exp2(m_hist[t] - stats[0]) * stats[1]
        p = e_buf[t] * factor
        ds = (p * (d_buf[t] - stats[2])).astype(BF16)
        out[1] = jnp.dot(p.astype(BF16), qg[1], preferred_element_type=F32)
        out[0] = jnp.dot(ds, qg[0], preferred_element_type=F32)
        dq_acc[...] += jnp.dot(kv[t, 0].T, ds, preferred_element_type=F32)

    def core_copy(far, d):
        return remote(to_core.at[far, d], got_core.at[far, d], c2_send.at[far, d], c2_recv.at[far, d], c_peer)

    def x_copy(a, d):
        return remote(to_x.at[d, a], got_x.at[d, a], x2_send.at[a, d], x2_recv.at[a, d], x_peer)

    def y_copy(a, d, src):
        return remote(src, cols(outs[a], y), y2_send.at[a, d], y2_recv.at[a, d], seq_id(x, y_of(d), c))

    def sum_far(d):
        arrived(got_core.at[0, d], c2_recv.at[0, d])
        to_x[d] = (keep[0, d] + got_core[0, d]).astype(BF16)

    def sum_near(d):
        arrived(got_core.at[1, d], c2_recv.at[1, d])
        keep[1, d] = keep[1, d] + got_core[1, d]

    def final_sum(a, d):
        arrived(got_x.at[d, a], x2_recv.at[a, d])
        total = keep[1, d, a] + got_x[d, a].astype(F32)
        return (total if a else total * SCALE).astype(BF16)

    def finish(a, d):
        final[d, a] = final_sum(a, d)
        y_copy(a + 1, d, final.at[d, a]).start()

    def distance(n):
        back = 3 - n
        return back + back // 2 - 2 * (back // 3)

    def b_far(n, carry):
        d = distance(n)
        pass_b(chunk(1 - x, y_of(d), 1 - c), to_core.at[0, d])
        core_copy(0, d).start()

        @pl.when(n == 1)
        def _():
            sum_far(2)
            for a in range(2):
                x_copy(a, 2).start()

        @pl.when(n == 2)
        def _():
            sum_far(3)
            x_copy(0, 3).start()

        @pl.when(n == 3)
        def _():
            sum_far(1)
            x_copy(0, 1).start()
            x_copy(1, 3).start()
            x_copy(1, 1).start()

        pass_b(chunk(1 - x, y_of(d), c), keep.at[0, d])
        return carry

    def b_near(n, carry):
        d = distance(n)
        pass_b(chunk(x, y_of(d), 1 - c), to_core.at[1, d])
        core_copy(1, d).start()

        @pl.when(n == 0)
        def _():
            sum_far(0)
            for a in range(2):
                x_copy(a, 0).start()

        @pl.when(n == 1)
        def _():
            sum_near(2)

        @pl.when(n == 2)
        def _():
            sum_near(3)
            finish(0, 2)

        @pl.when(n == 3)
        def _():
            sum_near(1)
            finish(1, 2)

        pass_b(chunk(x, y_of(d), c), keep.at[1, d])
        return carry

    lax.fori_loop(0, 4, b_far, 0)
    lax.fori_loop(0, 4, b_near, 0)

    for i in range(4):
        dq_low[i * ROWS : (i + 1) * ROWS] = (dq_acc[:, i * ROWS : (i + 1) * ROWS].T * SCALE).astype(BF16)
    for d in (2, 1, 3):
        y_copy(0, d, dq_low.at[rows(SLOT_OF[d])]).start()
    own_cols = pl.ds(pl.multiple_of(y * HD, HD), HD)
    dq_out[:, own_cols] = dq_low[:ROWS]
    sum_near(0)
    for a in range(2):
        finish(a, 3)
        finish(a, 1)
    for a in range(2):
        outs[a + 1][:, own_cols] = final_sum(a, 0)

    for d in (3, 2, 1):
        for a in range(3):
            arrived(cols(outs[a], y_of(d)), y2_recv.at[a, 4 - d])
    for copy in sends:
        copy.wait_send()
    for d in range(4):
        for a in range(2):
            sent(kv.at[0, 0], x_send.at[a, d])
            sent(kv.at[0, 0], c_send.at[0, a, d])
            sent(kv.at[0, 0], c_send.at[1, a, d])
            sent(to_x.at[d, a], x2_send.at[a, d])
        sent(to_core.at[0, d], c2_send.at[0, d])
        sent(to_core.at[1, d], c2_send.at[1, d])
    for d in (1, 2, 3):
        for a in range(3):
            sent(cols(outs[a], y), y2_send.at[a, d])


def store_kernel(dq, dk, dv, dq_out, dk_out, dv_out, done):
    copies = [
        pltpu.make_async_copy(src, dst, done.at[i])
        for i, (src, dst) in enumerate(((dq, dq_out), (dk, dk_out), (dv, dv_out)))
    ]
    for copy in copies:
        copy.start()
    for copy in copies:
        copy.wait()


def local(query, key_rows, value_rows, out_grad, sample_blocks):
    dma = pltpu.SemaphoreType.DMA
    vmem = pltpu.VMEM
    out = jax.ShapeDtypeStruct((ROWS, 4 * HD), BF16)
    grads = pl.pallas_call(
        kernel,
        out_shape=(out,) * 3,
        in_specs=[pl.BlockSpec(memory_space=pl.ANY)] * 5,
        out_specs=(pl.BlockSpec(memory_space=vmem),) * 3,
        scratch_shapes=[
            vmem((16, 2, ROWS, HD), BF16),
            vmem((2, QUERIES, HD), BF16),
            vmem((16, ROWS, QUERIES), F32),
            vmem((16, ROWS, QUERIES), F32),
            vmem((16, 1, QUERIES), F32),
            vmem((3, 1, QUERIES), F32),
            vmem((HD, QUERIES), F32),
            vmem((QUERIES, HD), BF16),
            vmem((2, 4, 2, ROWS, HD), F32),
            vmem((2, 4, 2, ROWS, HD), F32),
            vmem((2, 4, 2, ROWS, HD), F32),
            vmem((4, 2, ROWS, HD), BF16),
            vmem((4, 2, ROWS, HD), BF16),
            vmem((4, 2, ROWS, HD), BF16),
            pltpu.SMEM((3,), jnp.int32),
            dma((4, 4)), dma((4, 4)), dma((2, 4)), dma((2, 4)), dma((2, 2, 4)), dma((2, 2, 4)), dma((6,)),
            dma((2, 4)), dma((2, 4)), dma((2, 4)), dma((2, 4)), dma((3, 4)), dma((3, 4)),
        ],
        compiler_params=pltpu.CompilerParams(
            collective_id=0, has_side_effects=True, vmem_limit_bytes=60 << 20
        ),
        name="attention_grads",
    )(sample_blocks, query, key_rows, value_rows, out_grad)
    return pl.pallas_call(
        store_kernel,
        out_shape=(out,) * 3,
        in_specs=[pl.BlockSpec(memory_space=vmem)] * 3,
        out_specs=(pl.BlockSpec(memory_space=pl.ANY),) * 3,
        scratch_shapes=[dma((3,))],
        name="store",
    )(*grads)


def solution(mesh):
    spec = P("seq", "head")
    return jax.shard_map(
        local, mesh=mesh, in_specs=(spec, spec, spec, spec, P()), out_specs=(spec,) * 3, check_vma=False
    )
```

```python
import jax
import jax.numpy as jnp
from jax import lax
from jax.experimental import pallas as pl
from jax.experimental.pallas import tpu as pltpu
from jax.sharding import PartitionSpec as P

HD = 128
BLK = 128
ROWS = 256
QUERIES = 1024
SLOT_OF = {0: 0, 1: 1, 3: 2, 2: 3}
MESH = pl.DeviceIdType.MESH
SCALE = HD**-0.5
EXP2_SCALE = SCALE * 1.4426950408889634
MASKED = -1e30
BF16 = jnp.bfloat16
F32 = jnp.float32
NT = (((1,), (1,)), ((), ()))


def place():
    s = lax.axis_index("seq")
    return lax.div(s, 8), lax.rem(lax.div(s, 2), 4), lax.rem(s, 2)


def seq_id(x, y, c):
    return {"seq": x * 8 + y * 2 + c}


def chunk(x, y, c):
    return x * 8 + y * 2 + c


def cols(ref, head):
    return ref.at[:, pl.ds(pl.multiple_of(head * HD, HD), HD)]


def rows(i):
    return pl.ds(pl.multiple_of(i * ROWS, ROWS), ROWS)


def kernel(
    blocks, q, k, v, g, dq_out, dk_out, dv_out,
    kv, qg, e_buf, d_buf, m_hist, stats, dq_acc, dq_low,
    to_core, got_core, keep, to_x, got_x, final, ends,
    y_send, y_recv, x_send, x_recv, c_send, c_recv, own,
    c2_send, c2_recv, x2_send, x2_recv, y2_send, y2_recv,
):
    x, y, c = place()
    x_peer, c_peer = seq_id(1 - x, y, c), seq_id(x, y, 1 - c)
    outs = (dq_out, dk_out, dv_out)

    def y_of(d):
        return lax.rem(y + d, 4)

    def remote(src, dst, send, recv, device):
        return pltpu.make_async_remote_copy(
            src_ref=src, dst_ref=dst, send_sem=send, recv_sem=recv, device_id=device, device_id_type=MESH
        )

    def arrived(dst, recv):
        remote(dst, dst, own.at[0], recv, x_peer).wait_recv()

    def sent(src, send):
        remote(src, src, send, own.at[0], x_peer).wait_send()

    peers = [x_peer, c_peer] + [seq_id(x, y_of(d), c) for d in (1, 2, 3)]
    barrier = pltpu.get_barrier_semaphore()
    for peer in peers:
        pl.semaphore_signal(barrier, inc=1, device_id=peer, device_id_type=MESH)

    here = chunk(x, y, c)
    own_copies = [
        pltpu.make_async_copy(cols(k, y), kv.at[here, 0], own.at[1]),
        pltpu.make_async_copy(cols(v, y), kv.at[here, 1], own.at[2]),
        pltpu.make_async_copy(cols(q, y), qg.at[0, rows(0)], own.at[3]),
        pltpu.make_async_copy(cols(g, y), qg.at[1, rows(0)], own.at[4]),
        pltpu.make_async_copy(blocks, ends, own.at[5]),
    ]
    for copy in own_copies:
        copy.start()

    pl.semaphore_wait(barrier, len(peers))

    sends = []

    def go(copy):
        copy.start()
        sends.append(copy)

    def y_keys(a, d):
        src = cols((k, v)[a], y_of(d))
        go(remote(src, kv.at[here, a], y_send.at[a, d], y_recv.at[a, d], seq_id(x, y_of(d), c)))

    def y_queries(d):
        for a, ref in enumerate((q, g)):
            slot = qg.at[a, rows(SLOT_OF[4 - d])]
            go(remote(cols(ref, y_of(d)), slot, y_send.at[a + 2, d], y_recv.at[a + 2, d], seq_id(x, y_of(d), c)))

    def onward(a, d):
        there = kv.at[chunk(x, y_of(d), c), a]
        remote(there, there, x_send.at[a, d], x_recv.at[a, d], x_peer).start()
        remote(there, there, c_send.at[0, a, d], c_recv.at[0, a, d], c_peer).start()

    for a in range(2):
        for d in (1, 3):
            y_keys(a, d)
    for a in range(2):
        own_copies[a].wait()
        onward(a, 0)
    y_queries(1)
    y_queries(3)
    for a in range(2):
        y_keys(a, 2)
    y_queries(2)
    def half_of(far):
        return x + far * (1 - 2 * x)

    def keys_arrived(a, d):
        arrived(kv.at[chunk(x, y_of(d), c), a], y_recv.at[a, 4 - d])
        onward(a, d)

    def queries_arrived(d):
        for a in range(2):
            arrived(qg.at[a, rows(SLOT_OF[d])], y_recv.at[a + 2, 4 - d])

    def far_arrived(d):
        for a in range(2):
            far = kv.at[chunk(1 - x, y_of(d), c), a]
            arrived(far, x_recv.at[a, d])
            remote(far, far, c_send.at[1, a, d], c_recv.at[1, a, d], c_peer).start()

    def core_arrived(far, d):
        t = chunk(half_of(far), y_of(d), 1 - c)
        for a in range(2):
            arrived(kv.at[t, a], c_recv.at[far, a, d])
        return t

    for copy in own_copies[2:]:
        copy.wait()
    for a in range(2):
        for d in (3, 1):
            keys_arrived(a, d)
    far_arrived(0)

    end0 = ends[0]
    end1 = end0 + ends[1]
    lane = lax.broadcasted_iota(jnp.int32, (1, QUERIES), 1)
    slot = lane >> 8
    lane_y = (y + jnp.where(slot == 3, 2, jnp.where(slot == 2, 3, slot))) & 3
    lane_block = 16 * x + 2 * c + 4 * lane_y + ((lane >> 7) & 1)
    lane_seg = (lane_block >= end0).astype(jnp.int32) + (lane_block >= end1).astype(jnp.int32)
    stats[0] = jnp.full((1, QUERIES), MASKED, F32)
    stats[1] = jnp.zeros((1, QUERIES), F32)
    stats[2] = jnp.zeros((1, QUERIES), F32)

    def pass_a(t, slots):
        for i in slots:
            sl = slice(i * ROWS, (i + 1) * ROWS)
            s = lax.dot_general(kv[t, 0], qg[0, sl], NT, preferred_element_type=F32)
            d = lax.dot_general(kv[t, 1], qg[1, sl], NT, preferred_element_type=F32)
            m, l, r = stats[0, :, sl], stats[1, :, sl], stats[2, :, sl]
            halves = (slice(0, BLK), slice(BLK, ROWS))
            allowed = []
            new = m
            for h, half in enumerate(halves):
                key_block = 2 * t + h
                key_seg = (key_block >= end0).astype(jnp.int32) + (key_block >= end1).astype(jnp.int32)
                allowed.append(lane_seg[:, sl] == key_seg)
                top = jnp.max(s[half], axis=0, keepdims=True) * EXP2_SCALE
                new = jnp.maximum(new, jnp.where(allowed[h], top, MASKED))
            factor = jnp.exp2(m - new)
            l, r = l * factor, r * factor
            for h, half in enumerate(halves):
                top = jnp.where(allowed[h], new, -MASKED)
                e = jnp.exp2(s[half] * EXP2_SCALE - top)
                l = l + jnp.sum(e, axis=0, keepdims=True)
                r = r + jnp.sum(e * d[half], axis=0, keepdims=True)
                e_buf[t, half, sl] = e
            d_buf[t, :, sl] = d
            stats[0, :, sl], stats[1, :, sl], stats[2, :, sl] = new, l, r
            m_hist[t, :, sl] = new

    def early(n):
        far = n // 3
        return far, (n + n // 2) * (1 - far)

    def a_own(n, carry):
        far, d = early(n)
        pass_a(chunk(half_of(far), y_of(d), c), (0,))
        pass_a(core_arrived(far, d), (0,))
        return carry

    def a_first(n, carry):
        @pl.when(n == 3)
        def _():
            for a in range(2):
                keys_arrived(a, 2)

        far, d = early(n)
        pass_a(chunk(half_of(far), y_of(d), c), (1, 2))
        pass_a(chunk(half_of(far), y_of(d), 1 - c), (1, 2))
        return carry

    def a_second():
        for far, d in ((0, 0), (0, 1), (0, 3), (1, 0)):
            for core in (c, 1 - c):
                pass_a(chunk(half_of(far), y_of(d), core), (3,))

    def a_third(n, carry):
        @pl.when(n == 2)
        def _():
            far_arrived(2)

        far, d = (n + 2) // 3, 2 + n - 3 * (n // 2)
        pass_a(chunk(half_of(far), y_of(d), c), (0, 1, 2, 3))
        pass_a(core_arrived(far, d), (0, 1, 2, 3))
        return carry

    lax.fori_loop(0, 4, a_own, 0)
    queries_arrived(3)
    queries_arrived(1)
    lax.fori_loop(0, 4, a_first, 0)
    far_arrived(3)
    queries_arrived(2)
    a_second()
    far_arrived(1)
    lax.fori_loop(0, 4, a_third, 0)

    inv = 1.0 / stats[1]
    stats[2] = stats[2] * inv
    stats[1] = inv
    dq_acc[...] = jnp.zeros_like(dq_acc)

    def pass_b(t, out):
        factor = jnp.exp2(m_hist[t] - stats[0]) * stats[1]
        p = e_buf[t] * factor
        ds = (p * (d_buf[t] - stats[2])).astype(BF16)
        out[1] = jnp.dot(p.astype(BF16), qg[1], preferred_element_type=F32)
        out[0] = jnp.dot(ds, qg[0], preferred_element_type=F32)
        dq_acc[...] += jnp.dot(kv[t, 0].T, ds, preferred_element_type=F32)

    def core_copy(far, d):
        return remote(to_core.at[far, d], got_core.at[far, d], c2_send.at[far, d], c2_recv.at[far, d], c_peer)

    def x_copy(a, d):
        return remote(to_x.at[d, a], got_x.at[d, a], x2_send.at[a, d], x2_recv.at[a, d], x_peer)

    def y_copy(a, d, src):
        return remote(src, cols(outs[a], y), y2_send.at[a, d], y2_recv.at[a, d], seq_id(x, y_of(d), c))

    def sum_far(d):
        arrived(got_core.at[0, d], c2_recv.at[0, d])
        to_x[d] = (keep[0, d] + got_core[0, d]).astype(BF16)

    def sum_near(d):
        arrived(got_core.at[1, d], c2_recv.at[1, d])
        keep[1, d] = keep[1, d] + got_core[1, d]

    def final_sum(a, d):
        arrived(got_x.at[d, a], x2_recv.at[a, d])
        total = keep[1, d, a] + got_x[d, a].astype(F32)
        return (total if a else total * SCALE).astype(BF16)

    def finish(a, d):
        final[d, a] = final_sum(a, d)
        y_copy(a + 1, d, final.at[d, a]).start()

    def distance(n):
        back = 3 - n
        return back + back // 2 - 2 * (back // 3)

    def b_far(n, carry):
        d = distance(n)
        pass_b(chunk(1 - x, y_of(d), 1 - c), to_core.at[0, d])
        core_copy(0, d).start()

        @pl.when(n == 1)
        def _():
            sum_far(2)
            for a in range(2):
                x_copy(a, 2).start()

        @pl.when(n == 2)
        def _():
            sum_far(3)
            x_copy(0, 3).start()

        @pl.when(n == 3)
        def _():
            sum_far(1)
            x_copy(0, 1).start()
            x_copy(1, 3).start()
            x_copy(1, 1).start()

        pass_b(chunk(1 - x, y_of(d), c), keep.at[0, d])
        return carry

    def b_near(n, carry):
        d = distance(n)
        pass_b(chunk(x, y_of(d), 1 - c), to_core.at[1, d])
        core_copy(1, d).start()

        @pl.when(n == 0)
        def _():
            sum_far(0)
            for a in range(2):
                x_copy(a, 0).start()

        @pl.when(n == 1)
        def _():
            sum_near(2)

        @pl.when(n == 2)
        def _():
            sum_near(3)
            finish(0, 2)

        @pl.when(n == 3)
        def _():
            sum_near(1)
            finish(1, 2)

        pass_b(chunk(x, y_of(d), c), keep.at[1, d])
        return carry

    lax.fori_loop(0, 4, b_far, 0)
    lax.fori_loop(0, 4, b_near, 0)

    for i in range(4):
        dq_low[i * ROWS : (i + 1) * ROWS] = (dq_acc[:, i * ROWS : (i + 1) * ROWS].T * SCALE).astype(BF16)
    for d in (2, 1, 3):
        y_copy(0, d, dq_low.at[rows(SLOT_OF[d])]).start()
    own_cols = pl.ds(pl.multiple_of(y * HD, HD), HD)
    dq_out[:, own_cols] = dq_low[:ROWS]
    sum_near(0)
    for a in range(2):
        finish(a, 3)
        finish(a, 1)
    for a in range(2):
        outs[a + 1][:, own_cols] = final_sum(a, 0)

    for d in (3, 2, 1):
        for a in range(3):
            arrived(cols(outs[a], y_of(d)), y2_recv.at[a, 4 - d])
    for copy in sends:
        copy.wait_send()
    for d in range(4):
        for a in range(2):
            sent(kv.at[0, 0], x_send.at[a, d])
            sent(kv.at[0, 0], c_send.at[0, a, d])
            sent(kv.at[0, 0], c_send.at[1, a, d])
            sent(to_x.at[d, a], x2_send.at[a, d])
        sent(to_core.at[0, d], c2_send.at[0, d])
        sent(to_core.at[1, d], c2_send.at[1, d])
    for d in (1, 2, 3):
        for a in range(3):
            sent(cols(outs[a], y), y2_send.at[a, d])


def store_kernel(dq, dk, dv, dq_out, dk_out, dv_out, done):
    copies = [
        pltpu.make_async_copy(src, dst, done.at[i])
        for i, (src, dst) in enumerate(((dq, dq_out), (dk, dk_out), (dv, dv_out)))
    ]
    for copy in copies:
        copy.start()
    for copy in copies:
        copy.wait()


def local(query, key_rows, value_rows, out_grad, sample_blocks):
    dma = pltpu.SemaphoreType.DMA
    vmem = pltpu.VMEM
    out = jax.ShapeDtypeStruct((ROWS, 4 * HD), BF16)
    grads = pl.pallas_call(
        kernel,
        out_shape=(out,) * 3,
        in_specs=[pl.BlockSpec(memory_space=pl.ANY)] * 5,
        out_specs=(pl.BlockSpec(memory_space=vmem),) * 3,
        scratch_shapes=[
            vmem((16, 2, ROWS, HD), BF16),
            vmem((2, QUERIES, HD), BF16),
            vmem((16, ROWS, QUERIES), F32),
            vmem((16, ROWS, QUERIES), F32),
            vmem((16, 1, QUERIES), F32),
            vmem((3, 1, QUERIES), F32),
            vmem((HD, QUERIES), F32),
            vmem((QUERIES, HD), BF16),
            vmem((2, 4, 2, ROWS, HD), F32),
            vmem((2, 4, 2, ROWS, HD), F32),
            vmem((2, 4, 2, ROWS, HD), F32),
            vmem((4, 2, ROWS, HD), BF16),
            vmem((4, 2, ROWS, HD), BF16),
            vmem((4, 2, ROWS, HD), BF16),
            pltpu.SMEM((3,), jnp.int32),
            dma((4, 4)), dma((4, 4)), dma((2, 4)), dma((2, 4)), dma((2, 2, 4)), dma((2, 2, 4)), dma((6,)),
            dma((2, 4)), dma((2, 4)), dma((2, 4)), dma((2, 4)), dma((3, 4)), dma((3, 4)),
        ],
        compiler_params=pltpu.CompilerParams(
            collective_id=0, has_side_effects=True, vmem_limit_bytes=60 << 20
        ),
        name="attention_grads",
    )(sample_blocks, query, key_rows, value_rows, out_grad)
    return pl.pallas_call(
        store_kernel,
        out_shape=(out,) * 3,
        in_specs=[pl.BlockSpec(memory_space=vmem)] * 3,
        out_specs=(pl.BlockSpec(memory_space=pl.ANY),) * 3,
        scratch_shapes=[dma((3,))],
        name="store",
    )(*grads)


def solution(mesh):
    spec = P("seq", "head")
    return jax.shard_map(
        local, mesh=mesh, in_specs=(spec, spec, spec, spec, P()), out_specs=(spec,) * 3, check_vma=False
    )
```

```python
import jax
import jax.numpy as jnp
from jax import lax
from jax.experimental import pallas as pl
from jax.experimental.pallas import tpu as pltpu
from jax.sharding import PartitionSpec as P

HD = 128
BLK = 128
ROWS = 256
QUERIES = 1024
SLOT_OF = {0: 0, 1: 1, 3: 2, 2: 3}
MESH = pl.DeviceIdType.MESH
SCALE = HD**-0.5
EXP2_SCALE = SCALE * 1.4426950408889634
MASKED = -1e30
BF16 = jnp.bfloat16
F32 = jnp.float32
NT = (((1,), (1,)), ((), ()))


def place():
    s = lax.axis_index("seq")
    return lax.div(s, 8), lax.rem(lax.div(s, 2), 4), lax.rem(s, 2)


def seq_id(x, y, c):
    return {"seq": x * 8 + y * 2 + c}


def chunk(x, y, c):
    return x * 8 + y * 2 + c


def cols(ref, head):
    return ref.at[:, pl.ds(pl.multiple_of(head * HD, HD), HD)]


def rows(i):
    return pl.ds(pl.multiple_of(i * ROWS, ROWS), ROWS)


def kernel(
    blocks, q, k, v, g, dq_out, dk_out, dv_out,
    kv, qg, e_buf, d_buf, m_hist, stats, dq_acc, dq_low,
    to_core, got_core, keep, to_x, got_x, final, ends,
    y_send, y_recv, x_send, x_recv, c_send, c_recv, own,
    c2_send, c2_recv, x2_send, x2_recv, y2_send, y2_recv,
):
    x, y, c = place()
    x_peer, c_peer = seq_id(1 - x, y, c), seq_id(x, y, 1 - c)
    outs = (dq_out, dk_out, dv_out)

    def y_of(d):
        return lax.rem(y + d, 4)

    def remote(src, dst, send, recv, device):
        return pltpu.make_async_remote_copy(
            src_ref=src, dst_ref=dst, send_sem=send, recv_sem=recv, device_id=device, device_id_type=MESH
        )

    def arrived(dst, recv):
        remote(dst, dst, own.at[0], recv, x_peer).wait_recv()

    def sent(src, send):
        remote(src, src, send, own.at[0], x_peer).wait_send()

    peers = [x_peer, c_peer] + [seq_id(x, y_of(d), c) for d in (1, 2, 3)]
    barrier = pltpu.get_barrier_semaphore()
    for peer in peers:
        pl.semaphore_signal(barrier, inc=1, device_id=peer, device_id_type=MESH)

    here = chunk(x, y, c)
    own_copies = [
        pltpu.make_async_copy(cols(k, y), kv.at[here, 0], own.at[1]),
        pltpu.make_async_copy(cols(v, y), kv.at[here, 1], own.at[2]),
        pltpu.make_async_copy(cols(q, y), qg.at[0, rows(0)], own.at[3]),
        pltpu.make_async_copy(cols(g, y), qg.at[1, rows(0)], own.at[4]),
        pltpu.make_async_copy(blocks, ends, own.at[5]),
    ]
    for copy in own_copies:
        copy.start()

    pl.semaphore_wait(barrier, len(peers))

    sends = []

    def go(copy):
        copy.start()
        sends.append(copy)

    def y_keys(a, d):
        src = cols((k, v)[a], y_of(d))
        go(remote(src, kv.at[here, a], y_send.at[a, d], y_recv.at[a, d], seq_id(x, y_of(d), c)))

    def y_queries(d):
        for a, ref in enumerate((q, g)):
            slot = qg.at[a, rows(SLOT_OF[4 - d])]
            go(remote(cols(ref, y_of(d)), slot, y_send.at[a + 2, d], y_recv.at[a + 2, d], seq_id(x, y_of(d), c)))

    def onward(a, d):
        there = kv.at[chunk(x, y_of(d), c), a]
        remote(there, there, x_send.at[a, d], x_recv.at[a, d], x_peer).start()
        remote(there, there, c_send.at[0, a, d], c_recv.at[0, a, d], c_peer).start()

    for a in range(2):
        for d in (1, 3):
            y_keys(a, d)
    for a in range(2):
        own_copies[a].wait()
        onward(a, 0)
    y_queries(1)
    y_queries(3)
    for a in range(2):
        y_keys(a, 2)
    y_queries(2)
    def half_of(far):
        return x + far * (1 - 2 * x)

    def keys_arrived(a, d):
        arrived(kv.at[chunk(x, y_of(d), c), a], y_recv.at[a, 4 - d])
        onward(a, d)

    def queries_arrived(d):
        for a in range(2):
            arrived(qg.at[a, rows(SLOT_OF[d])], y_recv.at[a + 2, 4 - d])

    def far_arrived(d):
        for a in range(2):
            far = kv.at[chunk(1 - x, y_of(d), c), a]
            arrived(far, x_recv.at[a, d])
            remote(far, far, c_send.at[1, a, d], c_recv.at[1, a, d], c_peer).start()

    def core_arrived(far, d):
        t = chunk(half_of(far), y_of(d), 1 - c)
        for a in range(2):
            arrived(kv.at[t, a], c_recv.at[far, a, d])
        return t

    for copy in own_copies[2:]:
        copy.wait()
    for a in range(2):
        for d in (3, 1):
            keys_arrived(a, d)
    far_arrived(0)

    end0 = ends[0]
    end1 = end0 + ends[1]
    lane = lax.broadcasted_iota(jnp.int32, (1, QUERIES), 1)
    slot = lane >> 8
    lane_y = (y + jnp.where(slot == 3, 2, jnp.where(slot == 2, 3, slot))) & 3
    lane_block = 16 * x + 2 * c + 4 * lane_y + ((lane >> 7) & 1)
    lane_seg = (lane_block >= end0).astype(jnp.int32) + (lane_block >= end1).astype(jnp.int32)
    stats[0] = jnp.full((1, QUERIES), MASKED, F32)
    stats[1] = jnp.zeros((1, QUERIES), F32)
    stats[2] = jnp.zeros((1, QUERIES), F32)

    def pass_a(t, slots):
        for i in slots:
            sl = slice(i * ROWS, (i + 1) * ROWS)
            s = lax.dot_general(kv[t, 0], qg[0, sl], NT, preferred_element_type=F32)
            d = lax.dot_general(kv[t, 1], qg[1, sl], NT, preferred_element_type=F32)
            m, l, r = stats[0, :, sl], stats[1, :, sl], stats[2, :, sl]
            halves = (slice(0, BLK), slice(BLK, ROWS))
            allowed = []
            new = m
            for h, half in enumerate(halves):
                key_block = 2 * t + h
                key_seg = (key_block >= end0).astype(jnp.int32) + (key_block >= end1).astype(jnp.int32)
                allowed.append(lane_seg[:, sl] == key_seg)
                top = jnp.max(s[half], axis=0, keepdims=True) * EXP2_SCALE
                new = jnp.maximum(new, jnp.where(allowed[h], top, MASKED))
            factor = jnp.exp2(m - new)
            l, r = l * factor, r * factor
            for h, half in enumerate(halves):
                top = jnp.where(allowed[h], new, -MASKED)
                e = jnp.exp2(s[half] * EXP2_SCALE - top)
                l = l + jnp.sum(e, axis=0, keepdims=True)
                r = r + jnp.sum(e * d[half], axis=0, keepdims=True)
                e_buf[t, half, sl] = e
            d_buf[t, :, sl] = d
            stats[0, :, sl], stats[1, :, sl], stats[2, :, sl] = new, l, r
            m_hist[t, :, sl] = new

    def early(n):
        far = n // 3
        return far, (n + n // 2) * (1 - far)

    def a_own(n, carry):
        far, d = early(n)
        pass_a(chunk(half_of(far), y_of(d), c), (0,))
        pass_a(core_arrived(far, d), (0,))
        return carry

    def a_first(n, carry):
        @pl.when(n == 3)
        def _():
            for a in range(2):
                keys_arrived(a, 2)

        far, d = early(n)
        pass_a(chunk(half_of(far), y_of(d), c), (1, 2))
        pass_a(chunk(half_of(far), y_of(d), 1 - c), (1, 2))
        return carry

    def a_second():
        for far, d in ((0, 0), (0, 1), (0, 3), (1, 0)):
            for core in (c, 1 - c):
                pass_a(chunk(half_of(far), y_of(d), core), (3,))

    def a_third(n, carry):
        @pl.when(n == 1)
        def _():
            far_arrived(2)

        far, d = (n + 2) // 3, 2 + n - 3 * (n // 2)
        pass_a(chunk(half_of(far), y_of(d), c), (0, 1, 2, 3))
        pass_a(core_arrived(far, d), (0, 1, 2, 3))
        return carry

    lax.fori_loop(0, 4, a_own, 0)
    queries_arrived(3)
    queries_arrived(1)
    lax.fori_loop(0, 4, a_first, 0)
    far_arrived(3)
    queries_arrived(2)
    a_second()
    far_arrived(1)
    lax.fori_loop(0, 4, a_third, 0)

    inv = 1.0 / stats[1]
    stats[2] = stats[2] * inv
    stats[1] = inv
    dq_acc[...] = jnp.zeros_like(dq_acc)

    def pass_b(t, out):
        factor = jnp.exp2(m_hist[t] - stats[0]) * stats[1]
        p = e_buf[t] * factor
        ds = (p * (d_buf[t] - stats[2])).astype(BF16)
        out[1] = jnp.dot(p.astype(BF16), qg[1], preferred_element_type=F32)
        out[0] = jnp.dot(ds, qg[0], preferred_element_type=F32)
        dq_acc[...] += jnp.dot(kv[t, 0].T, ds, preferred_element_type=F32)

    def core_copy(far, d):
        return remote(to_core.at[far, d], got_core.at[far, d], c2_send.at[far, d], c2_recv.at[far, d], c_peer)

    def x_copy(a, d):
        return remote(to_x.at[d, a], got_x.at[d, a], x2_send.at[a, d], x2_recv.at[a, d], x_peer)

    def y_copy(a, d, src):
        return remote(src, cols(outs[a], y), y2_send.at[a, d], y2_recv.at[a, d], seq_id(x, y_of(d), c))

    def sum_far(d):
        arrived(got_core.at[0, d], c2_recv.at[0, d])
        to_x[d] = (keep[0, d] + got_core[0, d]).astype(BF16)

    def sum_near(d):
        arrived(got_core.at[1, d], c2_recv.at[1, d])
        keep[1, d] = keep[1, d] + got_core[1, d]

    def final_sum(a, d):
        arrived(got_x.at[d, a], x2_recv.at[a, d])
        total = keep[1, d, a] + got_x[d, a].astype(F32)
        return (total if a else total * SCALE).astype(BF16)

    def finish(a, d):
        final[d, a] = final_sum(a, d)
        y_copy(a + 1, d, final.at[d, a]).start()

    def distance(n):
        back = 3 - n
        return back + back // 2 - 2 * (back // 3)

    def b_far(n, carry):
        d = distance(n)
        pass_b(chunk(1 - x, y_of(d), 1 - c), to_core.at[0, d])
        core_copy(0, d).start()

        @pl.when(n == 1)
        def _():
            sum_far(2)
            for a in range(2):
                x_copy(a, 2).start()

        @pl.when(n == 2)
        def _():
            sum_far(3)
            x_copy(0, 3).start()

        @pl.when(n == 3)
        def _():
            sum_far(1)
            x_copy(0, 1).start()
            x_copy(1, 3).start()
            x_copy(1, 1).start()

        pass_b(chunk(1 - x, y_of(d), c), keep.at[0, d])
        return carry

    def b_near(n, carry):
        d = distance(n)
        pass_b(chunk(x, y_of(d), 1 - c), to_core.at[1, d])
        core_copy(1, d).start()

        @pl.when(n == 0)
        def _():
            sum_far(0)
            for a in range(2):
                x_copy(a, 0).start()

        @pl.when(n == 1)
        def _():
            sum_near(2)

        @pl.when(n == 2)
        def _():
            sum_near(3)
            finish(0, 2)

        @pl.when(n == 3)
        def _():
            sum_near(1)
            finish(1, 2)

        pass_b(chunk(x, y_of(d), c), keep.at[1, d])
        return carry

    lax.fori_loop(0, 4, b_far, 0)
    lax.fori_loop(0, 4, b_near, 0)

    for i in range(4):
        dq_low[i * ROWS : (i + 1) * ROWS] = (dq_acc[:, i * ROWS : (i + 1) * ROWS].T * SCALE).astype(BF16)
    for d in (2, 1, 3):
        y_copy(0, d, dq_low.at[rows(SLOT_OF[d])]).start()
    own_cols = pl.ds(pl.multiple_of(y * HD, HD), HD)
    dq_out[:, own_cols] = dq_low[:ROWS]
    sum_near(0)
    for a in range(2):
        finish(a, 3)
        finish(a, 1)
    for a in range(2):
        outs[a + 1][:, own_cols] = final_sum(a, 0)

    for d in (3, 2, 1):
        for a in range(3):
            arrived(cols(outs[a], y_of(d)), y2_recv.at[a, 4 - d])
    for copy in sends:
        copy.wait_send()
    for d in range(4):
        for a in range(2):
            sent(kv.at[0, 0], x_send.at[a, d])
            sent(kv.at[0, 0], c_send.at[0, a, d])
            sent(kv.at[0, 0], c_send.at[1, a, d])
            sent(to_x.at[d, a], x2_send.at[a, d])
        sent(to_core.at[0, d], c2_send.at[0, d])
        sent(to_core.at[1, d], c2_send.at[1, d])
    for d in (1, 2, 3):
        for a in range(3):
            sent(cols(outs[a], y), y2_send.at[a, d])


def store_kernel(dq, dk, dv, dq_out, dk_out, dv_out, done):
    copies = [
        pltpu.make_async_copy(src, dst, done.at[i])
        for i, (src, dst) in enumerate(((dq, dq_out), (dk, dk_out), (dv, dv_out)))
    ]
    for copy in copies:
        copy.start()
    for copy in copies:
        copy.wait()


def local(query, key_rows, value_rows, out_grad, sample_blocks):
    dma = pltpu.SemaphoreType.DMA
    vmem = pltpu.VMEM
    out = jax.ShapeDtypeStruct((ROWS, 4 * HD), BF16)
    grads = pl.pallas_call(
        kernel,
        out_shape=(out,) * 3,
        in_specs=[pl.BlockSpec(memory_space=pl.ANY)] * 5,
        out_specs=(pl.BlockSpec(memory_space=vmem),) * 3,
        scratch_shapes=[
            vmem((16, 2, ROWS, HD), BF16),
            vmem((2, QUERIES, HD), BF16),
            vmem((16, ROWS, QUERIES), F32),
            vmem((16, ROWS, QUERIES), F32),
            vmem((16, 1, QUERIES), F32),
            vmem((3, 1, QUERIES), F32),
            vmem((HD, QUERIES), F32),
            vmem((QUERIES, HD), BF16),
            vmem((2, 4, 2, ROWS, HD), F32),
            vmem((2, 4, 2, ROWS, HD), F32),
            vmem((2, 4, 2, ROWS, HD), F32),
            vmem((4, 2, ROWS, HD), BF16),
            vmem((4, 2, ROWS, HD), BF16),
            vmem((4, 2, ROWS, HD), BF16),
            pltpu.SMEM((3,), jnp.int32),
            dma((4, 4)), dma((4, 4)), dma((2, 4)), dma((2, 4)), dma((2, 2, 4)), dma((2, 2, 4)), dma((6,)),
            dma((2, 4)), dma((2, 4)), dma((2, 4)), dma((2, 4)), dma((3, 4)), dma((3, 4)),
        ],
        compiler_params=pltpu.CompilerParams(
            collective_id=0, has_side_effects=True, vmem_limit_bytes=60 << 20
        ),
        name="attention_grads",
    )(sample_blocks, query, key_rows, value_rows, out_grad)
    return pl.pallas_call(
        store_kernel,
        out_shape=(out,) * 3,
        in_specs=[pl.BlockSpec(memory_space=vmem)] * 3,
        out_specs=(pl.BlockSpec(memory_space=pl.ANY),) * 3,
        scratch_shapes=[dma((3,))],
        name="store",
    )(*grads)


def solution(mesh):
    spec = P("seq", "head")
    return jax.shard_map(
        local, mesh=mesh, in_specs=(spec, spec, spec, spec, P()), out_specs=(spec,) * 3, check_vma=False
    )
```
